128 devices in a mesh: fsdp: 16 (over x, z_lo, core), tp: 8 (over y, z_hi).
Axes of the slice: x: 4, y: 4, z: 4 (z_hi: 2, z_lo: 2; z = z_hi * 2 + z_lo), core: 2. Of those that a mesh axis runs over, the one named last changes fastest.
Arguments:
- acts: bfloat16 [6144, 8192], P('fsdp', 'tp'), may hold values from -6 to 6
- frozen: bfloat16 [8192, 8192], P('tp', 'fsdp'), may hold values from -0.0625 to 0.0625
- delta_tiles: bfloat16 [8, 64, 128, 128], P('tp', 'fsdp'), may hold values from -0.29882812 to 0.29882812
- delta_index: int32 [8, 64, 2], P('tp', 'fsdp'), may hold values from 0 to 63, as said below
- delta_count: int32 [8, 16], P('tp', 'fsdp'), may hold values from 1 to 4, as said below
- cotangent: bfloat16 [6144, 8192], P('fsdp', 'tp'), may hold values from -6 to 6
Outputs:
- output: bfloat16 [6144, 8192], P('fsdp', 'tp')
- grad_input: bfloat16 [6144, 8192], P('fsdp', 'tp')
- delta_grad: float32 [8, 64, 128, 128], P('tp', 'fsdp')
The draws below stay inside these ranges and needn't reach their ends.
Inputs may be any that keep to these rules, and one draw needn't show every extreme that they name: `delta_index`: in each head slice the 64 pairs are distinct, the first below 8 and the second below 64. `delta_count`: in each head slice exactly one owner has all 4 slots used.
All inputs are finite; a program needn't handle non-finite values.
Results may differ from the reference program's by a relative error of at most 0.001.
Values may be sent and summed in bfloat16 or wider, within the bound.
No kernel may reach another device: no remote copies, remote signals or barrier semaphores. Data moves between devices by JAX's collectives and lax.ppermute only.
A program may use at most 192 MiB of HBM per device.

```python
import jax
import jax.numpy as jnp
from jax import lax

D = 8192
TILE = 128
CAP = 4
TOKENS = 6144
RB = 8
CB = 64
SLOTS = 64
N_FSDP = 16
N_TP = 8


def draw_delta_index(key, part):
    key = jax.random.fold_in(key, 11)
    slice_keys = jax.random.split(key, N_TP)

    def one_slice(slice_key):
        pick_key, order_key = jax.random.split(slice_key)
        middle = 1 + jax.random.permutation(pick_key, RB * CB - 2)[:SLOTS - 2]
        ends = jnp.array([0, RB * CB - 1], dtype=jnp.int32)
        chosen = jnp.concatenate([ends, middle.astype(jnp.int32)])
        chosen = chosen[jax.random.permutation(order_key, SLOTS)]
        return jnp.stack([chosen // CB, chosen % CB], axis=-1).astype(jnp.int32)
    return jax.vmap(one_slice)(slice_keys)


def draw_delta_count(key, part):
    key = jax.random.fold_in(key, 23)
    first_key, second_key = jax.random.split(key)
    base = jax.random.randint(first_key, (N_TP, N_FSDP), 1, CAP)
    busiest = jax.random.randint(second_key, (N_TP,), 0, N_FSDP)
    full = jnp.arange(N_FSDP)[None, :] == busiest[:, None]
    return jnp.where(full, CAP, base).astype(jnp.int32)


def steps_of(key, shape, pieces, low, largest):
    def one(dim, shards_of):
        steps = jax.random.uniform(jax.random.fold_in(jax.random.fold_in(key, 6), dim), (shards_of,), jnp.float32, low / len(pieces), largest / len(pieces))
        return jnp.repeat(jnp.exp(steps), shape[dim] // shards_of).reshape((-1,) + (1,) * (len(shape) - dim - 1))

    gain = one(*pieces[0])
    for cut in pieces[1:]:
        gain = gain * one(*cut)
    return gain


def normal_values(rng, extent, deviation, most, cuts=(), kind=jnp.bfloat16):
    entries = jax.random.normal(rng, extent, jnp.float32) * deviation
    if len(cuts) > 0:
        entries = steps_of(rng, extent, cuts, -0.22, 0.18) * entries
    return jnp.clip(entries, min=-most, max=most).astype(kind)


def setup_inputs(seed: int = 0) -> dict:
    key_of = jax.random.split(jax.random.key(seed), 7)
    acts = normal_values(key_of[0], (TOKENS, D), 1.0, 6.0, ((0, 16), (1, 8)))
    frozen = normal_values(key_of[1], (D, D), D ** -0.5, 0.0625, ((0, 8), (1, 16)))
    delta_tiles = normal_values(key_of[2], (N_TP, SLOTS, TILE, TILE), 0.05, 0.29882812, ((0, 8), (1, 16)))
    delta_index = draw_delta_index(jax.random.fold_in(key_of[6], 71), 0)
    delta_count = draw_delta_count(jax.random.fold_in(key_of[6], 71), 0)
    cotangent = normal_values(key_of[5], (TOKENS, D), 1.0, 6.0, ((0, 16), (1, 8)))
    return {"acts": acts, "frozen": frozen, "delta_tiles": delta_tiles, "delta_index": delta_index, "delta_count": delta_count, "cotangent": cotangent}


def live_slots(delta_count):
    within = jnp.arange(SLOTS, dtype=jnp.int32) % CAP
    return within[None, :] < jnp.repeat(delta_count, CAP, axis=1)

def reference(acts, frozen, delta_tiles, delta_index, delta_count, cotangent):
    token_count = acts.shape[0]
    live = live_slots(delta_count)
    masked = delta_tiles * live[:, :, None, None].astype(jnp.bfloat16)
    scaling = 1.0 / jnp.sqrt(jnp.float32(token_count))
    act_slices = acts.reshape(token_count, N_TP, RB, TILE).transpose(1, 0, 2, 3)
    cot_blocks = cotangent.reshape(token_count, CB, TILE)

    def one_slice(extra_out, inputs):
        act_slice, tiles, index, live_row = inputs
        row_blocks = index[:, 0].astype(jnp.int32)
        col_blocks = index[:, 1].astype(jnp.int32)
        act_sel = act_slice[:, row_blocks].astype(jnp.float32)
        cot_sel = cot_blocks[:, col_blocks].astype(jnp.float32)
        tiles_wide = tiles.astype(jnp.float32)
        forward_terms = jnp.einsum('tsb,sbc->tsc', act_sel, tiles_wide)
        extra_out = extra_out.at[:, col_blocks].add(forward_terms)
        back_terms = jnp.einsum('tsc,sbc->tsb', cot_sel, tiles_wide)
        back_rows = jnp.zeros((token_count, RB, TILE), jnp.float32).at[:, row_blocks].add(back_terms)
        grads = jnp.einsum('tsb,tsc->sbc', act_sel, cot_sel) * scaling
        grads = grads * live_row[:, None, None].astype(jnp.float32)
        return (extra_out, (back_rows, grads))
    start_out = jnp.zeros((token_count, CB, TILE), jnp.float32)
    extra_out, stacked = lax.scan(one_slice, start_out, (act_slices, masked, delta_index, live))
    back_rows, delta_grad = stacked
    output = (jnp.dot(acts, frozen, preferred_element_type=jnp.float32) + extra_out.reshape(token_count, D)).astype(jnp.bfloat16)
    dense_back = lax.dot_general(cotangent, frozen, (((1,), (1,)), ((), ())), preferred_element_type=jnp.float32)
    grad_input = (dense_back + back_rows.transpose(1, 0, 2, 3).reshape(token_count, D)).astype(jnp.bfloat16)
    return (output, grad_input, delta_grad)
```

```python
import functools
import math

import jax
import jax.numpy as jnp
from jax import lax
from jax.experimental import pallas as pl
from jax.experimental.pallas import tpu as pltpu
from jax.sharding import Mesh, PartitionSpec as P

AXES = ("x", "zl", "core", "y", "zh")
RING = 4
CHUNKS = 2
EXTRA = 16
VMEM_LIMIT = 60 * 1024 * 1024


def shift(value, axis, step):
    return lax.ppermute(value, axis, [(i, (i + step) % RING) for i in range(RING)])


def swap(value, axis):
    return lax.ppermute(value, axis, [(0, 1), (1, 0)])


def dot(a, b):
    return jnp.dot(a, b, preferred_element_type=jnp.float32)


def dot_t(a, b):
    return lax.dot_general(a, b, (((1,), (1,)), ((), ())), preferred_element_type=jnp.float32)


def slot_place(where_ref, meta_ref, slot, per_owner, rows):
    x, zl, core, zh = (where_ref[i] for i in range(4))
    row, col, live = (meta_ref[3 * slot + i] for i in range(3))
    pair = lax.rem(slot // per_owner, 2)
    slice_zh = lax.rem(zh + pair, 2)
    group = col // 8
    within = lax.rem(col, 8)
    here = (live > 0) & (lax.rem(group, 2) == zh) & (within // 4 == core)
    relative = lax.rem(group // 2 + RING - x, RING)
    quarter = lax.rem(within, 4)
    col_block = (quarter // 2) * (2 * RING) + relative * 2 + lax.rem(quarter, 2)
    row_block = jnp.where(slice_zh == zl, rows, 0) + row
    return here, row_block, col_block


def build_kernel(per_owner, where_ref, meta_ref, tiles_ref, dense_ref):
    size = tiles_ref.shape[2]
    rows = dense_ref.shape[0] // size // 2

    def clear(i, carry):
        start = pl.multiple_of(i * size, size)
        dense_ref[pl.ds(start, size), :] = jnp.zeros((size, dense_ref.shape[1]), dense_ref.dtype)
        return carry

    lax.fori_loop(0, dense_ref.shape[0] // size, clear, 0)

    def place(slot, carry):
        here, row_block, col_block = slot_place(where_ref, meta_ref, slot, per_owner, rows)

        @pl.when(here)
        def _():
            r0 = pl.multiple_of(row_block * size, size)
            c0 = pl.multiple_of(col_block * size, size)
            dense_ref[pl.ds(r0, size), pl.ds(c0, size)] = tiles_ref[slot, :size, :]

        return carry

    lax.fori_loop(0, tiles_ref.shape[0], place, 0)


def grads_kernel(per_owner, where_ref, meta_ref, acts_ref, cot_ref, grads_ref):
    size = grads_ref.shape[1]
    slots = grads_ref.shape[0]
    rows = acts_ref.shape[1] // size // 2
    core = where_ref[2]

    def one(slot, carry):
        here, row_block, col_block = slot_place(where_ref, meta_ref, slot, per_owner, rows)
        owner = slot // (2 * per_owner)
        other = lax.rem(owner + core, 2)
        place = other * (slots // 2) + (owner // 2) * 2 * per_owner + lax.rem(slot, 2 * per_owner)

        @pl.when(here)
        def _():
            r0 = pl.multiple_of(row_block * size, size)
            c0 = pl.multiple_of(col_block * size, size)
            grads_ref[place] = lax.dot_general(
                acts_ref[:, pl.ds(r0, size)],
                cot_ref[:, pl.ds(c0, size)],
                (((0,), (0,)), ((), ())),
                preferred_element_type=jnp.float32,
            )

        @pl.when(jnp.logical_not(here))
        def _():
            grads_ref[place] = jnp.zeros((size, size), jnp.float32)

        return carry

    lax.fori_loop(0, slots, one, 0)


def smem():
    return pl.BlockSpec(memory_space=pltpu.SMEM)


def vmem():
    return pl.BlockSpec(memory_space=pltpu.VMEM)


def build_dense(where, meta, tiles, per_owner, height, width):
    return pl.pallas_call(
        functools.partial(build_kernel, per_owner),
        out_shape=jax.ShapeDtypeStruct((height, width), jnp.bfloat16),
        in_specs=[smem(), smem(), vmem()],
        out_specs=vmem(),
        compiler_params=pltpu.CompilerParams(vmem_limit_bytes=VMEM_LIMIT),
        cost_estimate=pl.CostEstimate(flops=0, bytes_accessed=16 * 1024 * 1024, transcendentals=0),
    )(where, meta, tiles)


def slot_grads(where, meta, acts, cot, per_owner, slots, size):
    return pl.pallas_call(
        functools.partial(grads_kernel, per_owner),
        out_shape=jax.ShapeDtypeStruct((slots, size, size), jnp.float32),
        in_specs=[smem(), smem(), vmem(), vmem()],
        out_specs=vmem(),
        compiler_params=pltpu.CompilerParams(vmem_limit_bytes=VMEM_LIMIT),
        cost_estimate=pl.CostEstimate(
            flops=slots * acts.shape[0] * size * size * 2, bytes_accessed=16 * 1024 * 1024, transcendentals=0
        ),
    )(where, meta, acts, cot)


def gather_x(block):
    half = block.shape[0] // 2
    before = shift(block, "x", 1)
    after = shift(block, "x", -1)
    far_top = shift(before[:half], "x", 1)
    far_bottom = shift(after[half:], "x", -1)
    far = jnp.concatenate([far_top, far_bottom], axis=0)
    return jnp.concatenate([block, after, far, before], axis=1)


def gather_y(block):
    half = block.shape[0] // 2
    before = shift(block, "y", 1)
    after = shift(block, "y", -1)
    far_top = shift(before[:half], "y", 1)
    far_bottom = shift(after[half:], "y", -1)
    far = jnp.concatenate([far_top, far_bottom], axis=0)
    return block, after, far, before


def scatter_y(take):
    far = take(2)
    half = far.shape[0] // 2
    from_before = shift(far[:half], "y", 1)
    from_after = shift(far[half:], "y", -1)
    up = take(1)
    down = take(3)
    up = jnp.concatenate([up[:half] + from_before, up[half:]], axis=0)
    down = jnp.concatenate([down[:half], down[half:] + from_after], axis=0)
    got_up = shift(up, "y", 1)
    got_down = shift(down, "y", -1)
    return take(0) + got_up + got_down


def local(acts, frozen, delta_tiles, delta_index, delta_count, cotangent):
    x, zl, core, y, zh = (lax.axis_index(a) for a in AXES)
    tokens, width = acts.shape
    per_owner, size = delta_tiles.shape[1], delta_tiles.shape[2]
    half_width = width // 2
    step = half_width // CHUNKS
    scaling = 1.0 / math.sqrt(tokens * RING * 4)
    where = jnp.stack([x, zl, core, zh]).astype(jnp.int32)

    live = jnp.arange(per_owner, dtype=jnp.int32) < delta_count[0, 0]
    info = jnp.concatenate([delta_index[0], live[:, None].astype(jnp.int32)], axis=1)
    info = jnp.pad(info[:, None, :], ((0, 0), (0, EXTRA - 1), (0, size - 3)))
    mine = jnp.concatenate([delta_tiles[0] * live[:, None, None].astype(jnp.bfloat16), info.astype(jnp.bfloat16)], axis=1)
    both = jnp.concatenate([mine, swap(mine, "zh")], axis=0)
    tiles = lax.all_gather(both, ("x", "zl", "core"), axis=0, tiled=True)
    meta = tiles[:, size, :3].astype(jnp.int32).reshape(-1)
    slots = tiles.shape[0]

    left, right = cotangent[:, :half_width], cotangent[:, half_width:]
    keep = jnp.where(core == 0, left, right)
    give = jnp.where(core == 0, right, left)
    cot_rows = jnp.concatenate([keep, swap(give, "core")], axis=0)
    cot_ring = gather_y(cot_rows)
    cot_ring = jnp.stack(cot_ring)
    cot_ring = [lax.dynamic_index_in_dim(cot_ring, (x + k - y) % RING, 0, keepdims=False) for k in range(RING)]
    cot = jnp.concatenate([c[:, j * step : (j + 1) * step] for j in range(CHUNKS) for c in cot_ring], axis=1)

    pieces = []
    for j in range(CHUNKS):
        own = frozen[:, j * step : (j + 1) * step]
        block_a = lax.ppermute(own, ("zl", "zh"), [(0, 2), (1, 0), (2, 3), (3, 1)])
        block_b = lax.ppermute(own, ("zl", "zh"), [(0, 0), (1, 2), (2, 1), (3, 3)])
        pieces.append(jnp.concatenate([block_a, block_b], axis=0))

    acts_other = swap(acts, "zh")
    own_is_b = zh == zl
    acts_a = jnp.where(own_is_b, acts_other, acts)
    acts_b = jnp.where(own_is_b, acts, acts_other)
    acts_both = jnp.concatenate([acts_a, acts_b], axis=1)
    acts_all = jnp.concatenate([acts_both, swap(acts_both, "core")], axis=0)

    dense = build_dense(where, meta, tiles, per_owner, 2 * width, 4 * half_width)
    out_delta = dot(acts_all, dense)
    back = dot_t(cot, dense)
    grads = slot_grads(where, meta, acts_all, cot, per_owner, slots, size)
    grads = grads[: slots // 2] + swap(grads[slots // 2 :], "core")
    grads = lax.psum_scatter(grads, ("x", "zl"), scatter_dimension=0, tiled=True)
    grads = grads[:per_owner] + swap(grads[per_owner:], "zh")
    delta_grad = (grads * scaling * live[:, None, None].astype(jnp.float32))[None]

    outs = []
    for j in range(CHUNKS):
        whole = gather_x(pieces[j])
        cols = slice(j * RING * step, (j + 1) * RING * step)
        part = dot(acts_all, whole) + out_delta[:, cols]
        back = back + dot_t(cot[:, cols], whole)

        def take(k, part=part):
            return lax.dynamic_slice_in_dim(part, ((y + k - x) % RING) * step, step, 1)

        outs.append(scatter_y(take))
    mine_out = jnp.concatenate(outs, axis=1).astype(jnp.bfloat16)
    kept, got = mine_out[:tokens], swap(mine_out[tokens:], "core")
    output = jnp.concatenate([jnp.where(core == 0, kept, got), jnp.where(core == 0, got, kept)], axis=1)

    back = back[:tokens] + swap(back[tokens:], "core")
    back_a, back_b = back[:, :width], back[:, width:]
    back_own = jnp.where(own_is_b, back_b, back_a)
    back_other = jnp.where(own_is_b, back_a, back_b)
    grad_input = (back_own + swap(back_other, "zh")).astype(jnp.bfloat16)
    return output, grad_input, delta_grad


def solution(mesh):
    fine = Mesh(mesh.devices.reshape(4, 2, 2, 4, 2), AXES)
    rows, cols = ("x", "zl", "core"), ("y", "zh")
    return jax.shard_map(
        local,
        mesh=fine,
        in_specs=(
            P(rows, cols),
            P(cols, rows),
            P(cols, rows, None, None),
            P(cols, rows, None),
            P(cols, rows),
            P(rows, cols),
        ),
        out_specs=(P(rows, cols), P(rows, cols), P(cols, rows, None, None)),
        check_vma=False,
    )
```

```python
import functools
import math

import jax
import jax.numpy as jnp
from jax import lax
from jax.experimental import pallas as pl
from jax.experimental.pallas import tpu as pltpu
from jax.sharding import Mesh, PartitionSpec as P

AXES = ("x", "zl", "core", "y", "zh")
RING = 4
CHUNKS = 2
EXTRA = 16
COST = 1000
VMEM_LIMIT = 60 * 1024 * 1024


def shift(value, axis, step):
    return lax.ppermute(value, axis, [(i, (i + step) % RING) for i in range(RING)])


def swap(value, axis):
    return lax.ppermute(value, axis, [(0, 1), (1, 0)])


def dot(a, b):
    return jnp.dot(a, b, preferred_element_type=jnp.float32)


def dot_t(a, b):
    return lax.dot_general(a, b, (((1,), (1,)), ((), ())), preferred_element_type=jnp.float32)


def slot_codes(where, info):
    x, zl, core, zh, _ = (where[i] for i in range(5))
    row, col, live = info[:, 0], info[:, 1], info[:, 2]
    slot = jnp.arange(info.shape[0], dtype=jnp.int32)
    slice_zh = zh ^ ((slot >> 2) & 1)
    here = (live > 0) & (((col >> 3) & 1) == zh) & (((col >> 2) & 1) == core)
    ring = ((col >> 4) + RING - x) & 3
    part = 1 - (slice_zh ^ zl)
    code = (part << 8) | (row << 5) | (((col >> 1) & 1) << 4) | (ring << 2) | (col & 1)
    return jnp.where(here, code, -1)


def slot_place(code):
    return code >> 8, (code >> 5) & 7, (code >> 4) & 1, (code >> 2) & 3, code & 1


def block_at(index, size):
    return pl.ds(pl.multiple_of(index * size, size), size)


def start_all(copies, sems):
    started = [pltpu.make_async_copy(source, target, sems.at[i]) for i, (source, target) in enumerate(copies)]
    for copy in started:
        copy.start()
    return started


def each_slot(codes_ref, tiles_ref, body):
    def one(slot, carry):
        code = codes_ref[slot]

        @pl.when(code >= 0)
        def _():
            body(slot_place(code), tiles_ref.at[slot])

        return carry

    lax.fori_loop(0, tiles_ref.shape[0], one, 0)


def clear(ref):
    def one(i, carry):
        ref[i] = jnp.zeros(ref.shape[1:], ref.dtype)
        return carry

    lax.fori_loop(0, ref.shape[0], one, 0)


def block_copies(refs, step, target_of):
    depth = refs[0].shape[0] if len(refs) == 8 else refs[0].shape[0] // 2
    copies = []
    for ring in range(RING):
        for part in range(2):
            if len(refs) == 8:
                source = refs[2 * ring + part]
            elif ring == 2:
                source = refs[2 + part]
            else:
                source = refs[(0, 1, None, 4)[ring]].at[pl.ds(part * depth, depth)]
            copies.append((source, target_of(part, ring)))
    return copies


def forward_kernel(chunk, where_ref, codes_ref, own_ref, other_ref, acts_ref, *refs):
    block_refs, rest = refs[:-10], refs[-10:]
    out_refs, (acts, tiles, blocks, sums, sems) = rest[:5], rest[5:]
    x, y = where_ref[0], where_ref[4]
    size = tiles.shape[2]
    step = sums.shape[2]
    depth = blocks.shape[1] // 2
    half = acts.shape[0] // 2
    rows = depth // size
    count = own_ref.shape[0]

    copies = [(acts_ref, acts), (own_ref, tiles.at[pl.ds(0, count)]), (other_ref, tiles.at[pl.ds(count, count)])]
    copies += block_copies(block_refs, step, lambda part, ring: blocks.at[ring, pl.ds(part * depth, depth)])
    started = start_all(copies, sems)
    clear(sums)
    for copy in started[:3]:
        copy.wait()

    def add(place, tile):
        part, row, where_chunk, ring, col = place

        @pl.when(where_chunk == chunk)
        def _():
            r, c = block_at(part * rows + row, size), block_at(col, size)
            sums[ring, :, c] += dot(acts[:, r], tile[:size, :])

    each_slot(codes_ref, tiles, add)
    mine_ref, up_ref, far_top_ref, far_bottom_ref, down_ref = out_refs

    def send(ring, targets):
        return [(sums.at[ring, pl.ds(first, length)], target) for first, length, target in targets]

    whole = 2 * half
    for ring in range(RING):
        started[3 + 2 * ring].wait()
        started[4 + 2 * ring].wait()
        sums[ring] += dot(acts[...], blocks[ring])
        place = (x + RING + ring - y) & 3

        @pl.when(place == 0)
        def _(ring=ring):
            start_all(send(ring, [(0, whole, mine_ref)]), sems)

        @pl.when(place == 1)
        def _(ring=ring):
            start_all(send(ring, [(0, whole, up_ref)]), sems.at[pl.ds(1, 1)])

        @pl.when(place == 2)
        def _(ring=ring):
            start_all(send(ring, [(0, half, far_top_ref), (half, half, far_bottom_ref)]), sems.at[pl.ds(11, 2)])

        @pl.when(place == 3)
        def _(ring=ring):
            start_all(send(ring, [(0, whole, down_ref)]), sems.at[pl.ds(2, 1)])

    finished = ((mine_ref, 0, whole), (up_ref, 1, whole), (down_ref, 2, whole), (far_top_ref, 11, half), (far_bottom_ref, 12, half))
    for target, sem, length in finished:
        pltpu.make_async_copy(sums.at[0, pl.ds(0, length)], target, sems.at[sem]).wait()


def grads_kernel(where_ref, codes_ref, acts_ref, cot_ref, own_ref, other_ref, grads, sems):
    size = grads.shape[1]
    half = own_ref.shape[0]
    rows = acts_ref.shape[1] // size // 2
    each = half // RING
    x = where_ref[0]

    def fill(first):
        def one(i, carry):
            code = codes_ref[first + i]
            place = first + ((i // each + x) & 3) * each + lax.rem(i, each)

            @pl.when(code >= 0)
            def _():
                part, row, chunk, ring, col = slot_place(code)
                grads[place] = lax.dot_general(
                    acts_ref[:, block_at(part * rows + row, size)],
                    cot_ref[(ring + x) & 3, :, block_at(2 * chunk + col, size)],
                    (((0,), (0,)), ((), ())),
                    preferred_element_type=jnp.float32,
                )

            @pl.when(code < 0)
            def _():
                grads[place] = jnp.zeros((size, size), jnp.float32)

            return carry

        lax.fori_loop(0, half, one, 0)

    fill(half)
    other_out = pltpu.make_async_copy(grads.at[pl.ds(half, half)], other_ref, sems.at[0])
    other_out.start()
    fill(0)
    own_out = pltpu.make_async_copy(grads.at[pl.ds(0, half)], own_ref, sems.at[1])
    own_out.start()
    other_out.wait()
    own_out.wait()


def backward_kernel(where_ref, codes_ref, own_ref, other_ref, cot_ref, *refs):
    block_refs, rest = refs[:-7], refs[-7:]
    (keep_ref, give_ref), (cot, tiles, blocks, sums, sems) = rest[:2], rest[2:]
    x, zl, zh = where_ref[0], where_ref[1], where_ref[3]
    size = tiles.shape[2]
    step = cot_ref.shape[2] // CHUNKS
    half = keep_ref.shape[1]
    count = own_ref.shape[0]

    def columns(chunk, ring):
        return pl.ds((chunk * RING + ring) * step, step)

    copies = []
    for chunk in range(CHUNKS):
        for ring in range(RING):
            source = cot_ref.at[(x + ring) & 3, :, pl.ds(chunk * step, step)]
            copies.append((source, cot.at[:, columns(chunk, ring)]))
    copies += [(own_ref, tiles.at[pl.ds(0, count)]), (other_ref, tiles.at[pl.ds(count, count)])]
    first = len(copies)
    for part in range(2):
        for chunk, chunk_refs in enumerate((block_refs[:5], block_refs[5:])):
            copies += block_copies(
                chunk_refs, step, lambda part, ring, chunk=chunk: blocks.at[part, :, columns(chunk, ring)]
            )[part::2]
    each = (len(copies) - first) // 2
    started = start_all(copies, sems)
    clear(sums)
    for copy in started[:first]:
        copy.wait()

    def add(place, tile):
        part, row, chunk, ring, col = place
        c = block_at(chunk * 2 * RING + ring * 2 + col, size)
        sums[part, :, block_at(row, size)] += dot_t(cot[:, c], tile[:size, :])

    each_slot(codes_ref, tiles, add)
    out = []
    for part in range(2):
        for copy in started[first + part * each : first + (part + 1) * each]:
            copy.wait()
        sums[part] += dot_t(cot[...], blocks[part])
        place = 1 - part ^ zl ^ zh
        out += start_all(
            [(sums.at[part, pl.ds(half, half)], give_ref.at[place]), (sums.at[part, pl.ds(0, half)], keep_ref.at[place])],
            sems.at[pl.ds(2 * part, 2)],
        )
    for copy in out:
        copy.wait()


def floats(*shape):
    return jax.ShapeDtypeStruct(shape, jnp.float32)


def call(kernel, outs, scalars, operands, scratch, flops, moved, space=pl.ANY):
    in_specs = [pl.BlockSpec(memory_space=pltpu.SMEM)] * len(scalars)
    in_specs += [pl.BlockSpec(memory_space=space)] * len(operands)
    return pl.pallas_call(
        kernel,
        out_shape=outs,
        in_specs=in_specs,
        out_specs=[pl.BlockSpec(memory_space=pl.ANY)] * len(outs),
        scratch_shapes=scratch,
        compiler_params=pltpu.CompilerParams(vmem_limit_bytes=VMEM_LIMIT),
        cost_estimate=pl.CostEstimate(flops=flops // COST, bytes_accessed=moved // COST, transcendentals=0),
    )(*scalars, *operands)


MIB = 1024 * 1024


def forward(chunk, scalars, tiles, acts, blocks, step):
    rows, width = acts.shape
    count, size = tiles[0].shape[0], tiles[0].shape[2]
    outs = [floats(rows, step)] * 2 + [floats(rows // 2, step)] * 2 + [floats(rows, step)]
    scratch = [
        pltpu.VMEM((rows, width), jnp.bfloat16),
        pltpu.VMEM((2 * count, *tiles[0].shape[1:]), jnp.bfloat16),
        pltpu.VMEM((RING, width, step), jnp.bfloat16),
        pltpu.VMEM((RING, rows, step), jnp.float32),
        pltpu.SemaphoreType.DMA((5 + 2 * RING,)),
    ]
    flops = 2 * RING * rows * width * step + 2 * count * rows * size * size
    operands = (*tiles, acts, *blocks)
    mine, up, far_top, far_bottom, down = call(
        functools.partial(forward_kernel, chunk), outs, scalars, operands, scratch, flops, 16 * MIB
    )
    return mine, up, far_top, far_bottom, down


def backward(scalars, tiles, cot, blocks_0, blocks_1, depth):
    rows, step = cot.shape[1], cot.shape[2] // CHUNKS
    count, size = tiles[0].shape[0], tiles[0].shape[2]
    width = CHUNKS * RING * step
    outs = [floats(2, rows // 2, depth)] * 2
    scratch = [
        pltpu.VMEM((rows, width), jnp.bfloat16),
        pltpu.VMEM((2 * count, *tiles[0].shape[1:]), jnp.bfloat16),
        pltpu.VMEM((2, depth, width), jnp.bfloat16),
        pltpu.VMEM((2, rows, depth), jnp.float32),
        pltpu.SemaphoreType.DMA((2 + 3 * CHUNKS * RING,)),
    ]
    flops = 4 * rows * depth * width + 2 * count * rows * size * size
    return call(backward_kernel, outs, scalars, (*tiles, cot, *blocks_0, *blocks_1), scratch, flops, 24 * MIB)


def slot_grads(scalars, acts, cot, count, size):
    outs = [floats(count, size, size)] * 2
    scratch = [pltpu.VMEM((2 * count, size, size), jnp.float32), pltpu.SemaphoreType.DMA((2,))]
    flops = 2 * count * acts.shape[0] * size * size
    return call(grads_kernel, outs, scalars, (acts, cot), scratch, flops, 16 * MIB, pltpu.VMEM)


def tie(*values):
    return lax.optimization_barrier(values)


def near(block, axis):
    return shift(block, axis, -1), shift(block, axis, 1)


def far(following, previous, axis):
    half = following.shape[0] // 2
    top = shift(previous[:half], axis, 1)
    bottom = shift(following[half:], axis, -1)
    return top, bottom


def scatter_near(up, down, got, axis):
    from_before, from_after = got
    half = up.shape[0] // 2
    up = jnp.concatenate([up[:half] + from_before, up[half:]], axis=0)
    down = jnp.concatenate([down[:half], down[half:] + from_after], axis=0)
    return shift(up, axis, 1), shift(down, axis, -1)


def local(acts, frozen, delta_tiles, delta_index, delta_count, cotangent):
    x, zl, core, y, zh = (lax.axis_index(a) for a in AXES)
    tokens, width = acts.shape
    per_owner, size = delta_tiles.shape[1], delta_tiles.shape[2]
    half_width = width // 2
    step = half_width // CHUNKS
    scaling = 1.0 / math.sqrt(tokens * RING * 4)
    where = jnp.stack([x, zl, core, zh, y]).astype(jnp.int32)
    own_is_b = zh == zl

    left, right = cotangent[:, :half_width], cotangent[:, half_width:]
    keep = jnp.where(core == 0, left, right)
    give = jnp.where(core == 0, right, left)

    def along_z(block):
        part_0 = lax.ppermute(block, ("zl", "zh"), [(0, 2), (1, 0), (2, 3), (3, 1)])
        part_1 = lax.ppermute(block, ("zl", "zh"), [(1, 2), (2, 1)])
        return part_0, part_1

    def parts(block, pair):
        return pair[0], jnp.where(own_is_b, block, pair[1])

    live = jnp.arange(per_owner, dtype=jnp.int32) < delta_count[0, 0]
    info = jnp.concatenate([delta_index[0], live[:, None].astype(jnp.int32)], axis=1)
    info = jnp.pad(info[:, None, :], ((0, 0), (0, EXTRA - 1), (0, size - 3)))
    mine = jnp.concatenate([delta_tiles[0] * live[:, None, None].astype(jnp.bfloat16), info.astype(jnp.bfloat16)], axis=1)

    frozen_0, frozen_1 = frozen[:, :step], frozen[:, step:]
    wide_1 = lax.all_gather(frozen_1, "x")
    got_z = along_z(frozen_0)
    cot_got = swap(give, "core")
    pair = jnp.concatenate([mine, swap(mine, "zh")], axis=0)
    other_pair = swap(pair, "zl")
    acts, keep, cot_got, frozen_0, got_z, pair, other_pair, frozen_1 = tie(
        acts, keep, cot_got, frozen_0, got_z, pair, other_pair, frozen_1
    )

    piece_0 = jnp.concatenate(parts(frozen_0, got_z), axis=0)
    quad = jnp.concatenate([jnp.where(zl == 0, pair, other_pair), jnp.where(zl == 0, other_pair, pair)], axis=0)
    quad_next, quad_prev = near(quad, "x")
    next_0, prev_0 = near(piece_0, "x")
    acts_other = swap(acts, "zh")
    acts_other, frozen_1 = tie(acts_other, frozen_1)
    got_z = [along_z(frozen_1)]
    cot_rows, wide_1 = tie(jnp.concatenate([keep, cot_got], axis=0), wide_1)
    cot = lax.all_gather(cot_rows, "y")
    quad, quad_next, quad_prev, piece_0, next_0, prev_0, acts, acts_other, frozen_1, got_z, wide_1 = tie(
        quad, quad_next, quad_prev, piece_0, next_0, prev_0, acts, acts_other, frozen_1, got_z, wide_1
    )

    turned_1 = [lax.dynamic_index_in_dim(wide_1, (x + k) % RING, 0, keepdims=False) for k in range(1, RING)]
    quad_far = far(quad_next, quad_prev, "x")
    far_0 = far(next_0, prev_0, "x")
    got_z += [along_z(turned_1[0])]
    quad, quad_next, quad_far, quad_prev, far_0, got_z, turned_1, acts, acts_other = tie(
        quad, quad_next, quad_far, quad_prev, far_0, got_z, turned_1, acts, acts_other
    )

    tiles = jnp.concatenate([quad, quad_next, *quad_far, quad_prev], axis=0)
    other_tiles = swap(tiles, "core")
    acts_a = jnp.where(own_is_b, acts_other, acts)
    acts_b = jnp.where(own_is_b, acts, acts_other)
    acts_both = jnp.concatenate([acts_a, acts_b], axis=1)
    acts_all = jnp.concatenate([acts_both, swap(acts_both, "core")], axis=0)
    info = jnp.concatenate([tiles[:, size, :3], other_tiles[:, size, :3]], axis=0).astype(jnp.int32)
    codes = slot_codes(where, info)
    slots = codes.shape[0]
    got_z += [along_z(turned_1[1])]
    tiles, other_tiles, codes, got_z, turned_1, acts_all, cot, frozen_1 = tie(
        tiles, other_tiles, codes, got_z, turned_1, acts_all, cot, frozen_1
    )

    scalars, tiles = (where, codes), (tiles, other_tiles)
    own_grads, other_grads = slot_grads(scalars, acts_all, cot, slots // 2, size)
    got_z += [along_z(turned_1[2])]
    blocks_0 = (piece_0, next_0, *far_0, prev_0)
    own_grads, other_grads, got_z, acts_all = tie(own_grads, other_grads, got_z, acts_all)
    blocks_1 = [part for block, pair in zip([frozen_1, *turned_1], got_z, strict=True) for part in parts(block, pair)]

    swapped_grads = swap(other_grads, "core")
    mine_0, up_0, far_top, far_bottom, down_0 = forward(0, scalars, tiles, acts_all, blocks_0, step)
    mine_0, far_top, far_bottom, own_grads, swapped_grads, cot = tie(
        mine_0, far_top, far_bottom, own_grads, swapped_grads, cot
    )

    def slab(k):
        place = ((x + k) % RING) * (slots // 8)
        return lax.dynamic_slice_in_dim(own_grads, place, slots // 8, 0) + lax.dynamic_slice_in_dim(
            swapped_grads, place, slots // 8, 0
        )

    got_0 = shift(far_top, "y", 1), shift(far_bottom, "y", -1)
    eighth = slots // 16
    far_slab = slab(2)
    got_g = shift(far_slab[:eighth], "x", 1), shift(far_slab[eighth:], "x", -1)
    keep, give = backward(scalars, tiles, cot, blocks_0, blocks_1, width)
    keep, give, got_0, got_g, acts_all, own_grads, swapped_grads = tie(
        keep, give, got_0, got_g, acts_all, own_grads, swapped_grads
    )

    given = swap(give, "core")
    got_0 = scatter_near(up_0, down_0, got_0, "y")
    got_g = scatter_near(slab(1), slab(3), got_g, "x")
    keep, given, acts_all = tie(keep, given, acts_all)

    back_own, back_other = keep[0] + given[0], keep[1] + given[1]
    middle = back_other.shape[0] // 2
    back_got_0 = swap(back_other[:middle], "zh")
    mine_1, up_1, far_top, far_bottom, down_1 = forward(1, scalars, tiles, acts_all, blocks_1, step)
    mine_1, far_top, far_bottom, got_0, back_got_0, back_other = tie(
        mine_1, far_top, far_bottom, got_0, back_got_0, back_other
    )

    got_1 = shift(far_top, "y", 1), shift(far_bottom, "y", -1)
    back_got_1 = swap(back_other[middle:], "zh")
    got_1, back_got_1, got_g = tie(got_1, back_got_1, got_g)
    got_1 = scatter_near(up_1, down_1, got_1, "y")
    out_0 = mine_0 + got_0[0] + got_0[1]
    out_1 = mine_1 + got_1[0] + got_1[1]

    grads = slab(0) + got_g[0] + got_g[1]
    grads_zl = grads.reshape(2, -1, size, size)
    grads = lax.dynamic_index_in_dim(grads_zl, zl, 0, keepdims=False) + swap(
        lax.dynamic_index_in_dim(grads_zl, 1 - zl, 0, keepdims=False), "zl"
    )
    grads = grads[:per_owner] + swap(grads[per_owner:], "zh")
    delta_grad = (grads * scaling * live[:, None, None].astype(jnp.float32))[None]

    mine_out = jnp.concatenate([out_0, out_1], axis=1).astype(jnp.bfloat16)
    kept, got = mine_out[:tokens], swap(mine_out[tokens:], "core")
    output = jnp.concatenate([jnp.where(core == 0, kept, got), jnp.where(core == 0, got, kept)], axis=1)
    grad_input = (back_own + jnp.concatenate([back_got_0, back_got_1], axis=0)).astype(jnp.bfloat16)
    return output, grad_input, delta_grad


def solution(mesh):
    fine = Mesh(mesh.devices.reshape(4, 2, 2, 4, 2), AXES)
    rows, cols = ("x", "zl", "core"), ("y", "zh")
    return jax.shard_map(
        local,
        mesh=fine,
        in_specs=(
            P(rows, cols),
            P(cols, rows),
            P(cols, rows, None, None),
            P(cols, rows, None),
            P(cols, rows),
            P(rows, cols),
        ),
        out_specs=(P(rows, cols), P(rows, cols), P(cols, rows, None, None)),
        check_vma=False,
    )
```

```python
import functools
import math

import jax
import jax.numpy as jnp
from jax import lax
from jax.experimental import pallas as pl
from jax.experimental.pallas import tpu as pltpu
from jax.sharding import Mesh, PartitionSpec as P

AXES = ("x", "zl", "core", "y", "zh")
RING = 4
CHUNKS = 2
EXTRA = 16
COST = 1000
VMEM_LIMIT = 60 * 1024 * 1024


def shift(value, axis, step):
    return lax.ppermute(value, axis, [(i, (i + step) % RING) for i in range(RING)])


def swap(value, axis):
    return lax.ppermute(value, axis, [(0, 1), (1, 0)])


def dot(a, b):
    return jnp.dot(a, b, preferred_element_type=jnp.float32)


def dot_t(a, b):
    return lax.dot_general(a, b, (((1,), (1,)), ((), ())), preferred_element_type=jnp.float32)


def slot_codes(where, info):
    x, zl, core, zh, _ = (where[i] for i in range(5))
    row, col, live = info[:, 0], info[:, 1], info[:, 2]
    slot = jnp.arange(info.shape[0], dtype=jnp.int32)
    slice_zh = zh ^ ((slot >> 2) & 1)
    here = (live > 0) & (((col >> 3) & 1) == zh) & (((col >> 2) & 1) == core)
    ring = ((col >> 4) + RING - x) & 3
    part = 1 - (slice_zh ^ zl)
    code = (part << 8) | (row << 5) | (((col >> 1) & 1) << 4) | (ring << 2) | (col & 1)
    return jnp.where(here, code, -1)


def slot_place(code):
    return code >> 8, (code >> 5) & 7, (code >> 4) & 1, (code >> 2) & 3, code & 1


def block_at(index, size):
    return pl.ds(pl.multiple_of(index * size, size), size)


def start_all(copies, sems):
    started = []
    for i, (source, target, *choice) in enumerate(copies):
        copy = pltpu.make_async_copy(source, target, sems.at[i])
        if choice:
            flag, instead = choice
            pl.when(flag)(pltpu.make_async_copy(instead, target, sems.at[i]).start)
            pl.when(jnp.logical_not(flag))(copy.start)
        else:
            copy.start()
        started.append(copy)
    return started


def each_slot(codes_ref, tiles_ref, body):
    def one(slot, carry):
        code = codes_ref[slot]

        @pl.when(code >= 0)
        def _():
            body(slot_place(code), tiles_ref[slot])

        return carry

    lax.fori_loop(0, tiles_ref.shape[0], one, 0)


def block_copies(where_ref, refs, target_of):
    same = where_ref[1] == where_ref[3]
    copies = []
    for ring in range(RING):
        for part in range(2):
            target = target_of(part, ring)
            if len(refs) == 3:
                got = refs[1 + part].at[ring]
                copies.append((got, target, same, refs[0].at[ring]) if part == 1 else (got, target))
            elif ring == 2:
                copies.append((refs[2 + part], target))
            else:
                depth = target.shape[0]
                copies.append((refs[(0, 1, None, 4)[ring]].at[pl.ds(part * depth, depth)], target))
    return copies


def acts_copies(where_ref, refs, acts):
    own = 1 - where_ref[3] ^ where_ref[1]
    acts_ref, other_ref, swapped_ref = refs
    tokens, depth = acts_ref.shape
    rows = pl.ds(0, tokens), pl.ds(tokens, tokens)
    cols = [pl.ds(pl.multiple_of(part * depth, depth), depth) for part in (own, 1 - own)]
    return [
        (acts_ref, acts.at[rows[0], cols[0]]),
        (other_ref, acts.at[rows[0], cols[1]]),
        (swapped_ref.at[0], acts.at[rows[1], cols[0]]),
        (swapped_ref.at[1], acts.at[rows[1], cols[1]]),
    ]


def forward_kernel(where_ref, codes_ref, tiles_ref, *refs):
    acts_refs, blocks_0, blocks_1, rest = refs[:3], refs[3:8], refs[8:-10], refs[-10:]
    out_refs, (acts, tiles, blocks, sums, sems) = rest[:5], rest[5:]
    x, y = where_ref[0], where_ref[4]
    size = tiles.shape[2]
    step = sums.shape[2] // CHUNKS
    depth = blocks.shape[2] // 2
    half = acts.shape[0] // 2

    copies = acts_copies(where_ref, acts_refs, acts)
    first = len(copies)
    for chunk, chunk_refs in enumerate((blocks_0, blocks_1)):
        copies += block_copies(
            where_ref, chunk_refs, lambda part, ring, chunk=chunk: blocks.at[chunk, ring, pl.ds(part * depth, depth)]
        )
    copies.append((tiles_ref.at[:, pl.ds(0, size)], tiles))
    started = start_all(copies, sems)
    for copy in started[:first]:
        copy.wait()
    for chunk in range(CHUNKS):
        cols = slice(chunk * step, (chunk + 1) * step)
        for ring in range(RING):
            for i in range(2):
                started[first + (chunk * RING + ring) * 2 + i].wait()
            sums[ring, :, cols] = dot(acts[...], blocks[chunk, ring])
    started[-1].wait()

    def add(place, tile):
        part, row, chunk, ring, col = place
        r, c = block_at(part * (depth // size) + row, size), block_at(chunk * (step // size) + col, size)
        sums[ring, :, c] += dot(acts[:, r], tile)

    each_slot(codes_ref, tiles, add)
    mine_ref, up_ref, far_top_ref, far_bottom_ref, down_ref = out_refs

    def ring_of(place):
        return (y - x + RING + place) & 3

    out = start_all(
        [
            (sums.at[ring_of(2), pl.ds(0, half)], far_top_ref),
            (sums.at[ring_of(2), pl.ds(half, half)], far_bottom_ref),
            (sums.at[ring_of(1)], up_ref),
            (sums.at[ring_of(3)], down_ref),
            (sums.at[ring_of(0)], mine_ref),
        ],
        sems,
    )
    for copy in out:
        copy.wait()


def grads_kernel(where_ref, codes_ref, *refs):
    acts_refs, (cot_ref, own_ref, other_ref, acts, cot, grads, sems) = refs[:3], refs[3:]
    size = grads.shape[1]
    half = own_ref.shape[0]
    rows = acts.shape[1] // size // 2
    x, core, y = where_ref[0], where_ref[2], where_ref[4]
    for copy in start_all(acts_copies(where_ref, acts_refs, acts) + [(cot_ref, cot)], sems):
        copy.wait()

    def fill(owner_core, first):
        def one(i, carry):
            code = codes_ref[((i >> 3) << 4) + (owner_core << 3) + (i & 7)]

            @pl.when(code >= 0)
            def _():
                part, row, chunk, ring, col = slot_place(code)
                grads[first + i] = lax.dot_general(
                    acts[:, block_at(part * rows + row, size)],
                    cot[(ring + x + RING - y) & 3, :, block_at(2 * chunk + col, size)],
                    (((0,), (0,)), ((), ())),
                    preferred_element_type=jnp.float32,
                )

            @pl.when(code < 0)
            def _():
                grads[first + i] = jnp.zeros((size, size), jnp.float32)

            return carry

        lax.fori_loop(0, half, one, 0)

    fill(1 - core, half)
    other_out = pltpu.make_async_copy(grads.at[pl.ds(half, half)], other_ref, sems.at[0])
    other_out.start()
    fill(core, 0)
    own_out = pltpu.make_async_copy(grads.at[pl.ds(0, half)], own_ref, sems.at[1])
    own_out.start()
    other_out.wait()
    own_out.wait()


def backward_kernel(where_ref, codes_ref, tiles_ref, cot_ref, *refs):
    blocks_0, blocks_1, rest = refs[:5], refs[5:-7], refs[-7:]
    (keep_ref, give_ref), (cot, tiles, blocks, sums, sems) = rest[:2], rest[2:]
    x, zl, zh, y = where_ref[0], where_ref[1], where_ref[3], where_ref[4]
    size = tiles.shape[2]
    step = cot_ref.shape[2] // CHUNKS
    half = keep_ref.shape[1]

    def columns(chunk, ring):
        return pl.ds((chunk * RING + ring) * step, step)

    copies = []
    for chunk in range(CHUNKS):
        for ring in range(RING):
            source = cot_ref.at[(x + ring + RING - y) & 3, :, pl.ds(chunk * step, step)]
            copies.append((source, cot.at[:, columns(chunk, ring)]))
    first = len(copies)
    for part in range(2):
        for chunk, chunk_refs in enumerate((blocks_0, blocks_1)):
            copies += block_copies(
                where_ref, chunk_refs, lambda part, ring, chunk=chunk: blocks.at[part, :, columns(chunk, ring)]
            )[part::2]
    copies.append((tiles_ref.at[:, pl.ds(0, size)], tiles))
    each = CHUNKS * RING
    started = start_all(copies, sems)
    for copy in started[:first]:
        copy.wait()
    for part in range(2):
        for copy in started[first + part * each : first + (part + 1) * each]:
            copy.wait()
        sums[part] = dot_t(cot[...], blocks[part])
    started[-1].wait()

    def add(place, tile):
        part, row, chunk, ring, col = place
        c = block_at(chunk * 2 * RING + ring * 2 + col, size)
        sums[part, :, block_at(row, size)] += dot_t(cot[:, c], tile)

    each_slot(codes_ref, tiles, add)
    out = []
    for part in range(2):
        place = 1 - part ^ zl ^ zh
        out += start_all(
            [(sums.at[part, pl.ds(half, half)], give_ref.at[place]), (sums.at[part, pl.ds(0, half)], keep_ref.at[place])],
            sems.at[pl.ds(2 * part, 2)],
        )
    for copy in out:
        copy.wait()


def floats(*shape):
    return jax.ShapeDtypeStruct(shape, jnp.float32)


def call(kernel, outs, scalars, operands, scratch, flops, moved):
    in_specs = [pl.BlockSpec(memory_space=pltpu.SMEM)] * len(scalars)
    in_specs += [pl.BlockSpec(memory_space=pl.ANY)] * len(operands)
    return pl.pallas_call(
        kernel,
        out_shape=outs,
        in_specs=in_specs,
        out_specs=[pl.BlockSpec(memory_space=pl.ANY)] * len(outs),
        scratch_shapes=scratch,
        compiler_params=pltpu.CompilerParams(vmem_limit_bytes=VMEM_LIMIT),
        cost_estimate=pl.CostEstimate(flops=flops // COST, bytes_accessed=moved // COST, transcendentals=0),
    )(*scalars, *operands)


MIB = 1024 * 1024


def forward(scalars, tiles, acts, blocks_0, blocks_1, step):
    rows, depth = 2 * acts[0].shape[0], acts[0].shape[1]
    count, size = tiles.shape[0], tiles.shape[2]
    width = CHUNKS * step
    outs = [floats(rows, width)] * 2 + [floats(rows // 2, width)] * 2 + [floats(rows, width)]
    scratch = [
        pltpu.VMEM((rows, 2 * depth), jnp.bfloat16),
        pltpu.VMEM((count, size, size), jnp.bfloat16),
        pltpu.VMEM((CHUNKS, RING, 2 * depth, step), jnp.bfloat16),
        pltpu.VMEM((RING, rows, width), jnp.float32),
        pltpu.SemaphoreType.DMA((5 + 2 * CHUNKS * RING,)),
    ]
    flops = 4 * RING * rows * depth * width + count * rows * size * size
    operands = (tiles, *acts, *blocks_0, *blocks_1)
    return call(forward_kernel, outs, scalars, operands, scratch, flops, 24 * MIB)


def backward(scalars, tiles, cot, blocks_0, blocks_1, depth):
    rows, step = cot.shape[1], cot.shape[2] // CHUNKS
    count, size = tiles.shape[0], tiles.shape[2]
    width = CHUNKS * RING * step
    outs = [floats(2, rows // 2, depth)] * 2
    scratch = [
        pltpu.VMEM((rows, width), jnp.bfloat16),
        pltpu.VMEM((count, size, size), jnp.bfloat16),
        pltpu.VMEM((2, depth, width), jnp.bfloat16),
        pltpu.VMEM((2, rows, depth), jnp.float32),
        pltpu.SemaphoreType.DMA((1 + 3 * CHUNKS * RING,)),
    ]
    flops = 4 * rows * depth * width + count * rows * size * size
    return call(backward_kernel, outs, scalars, (tiles, cot, *blocks_0, *blocks_1), scratch, flops, 24 * MIB)


def slot_grads(scalars, acts, cot, count, size):
    outs = [floats(count, size, size)] * 2
    scratch = [
        pltpu.VMEM((cot.shape[1], 2 * acts[0].shape[1]), jnp.bfloat16),
        pltpu.VMEM(cot.shape, jnp.bfloat16),
        pltpu.VMEM((2 * count, size, size), jnp.float32),
        pltpu.SemaphoreType.DMA((5,)),
    ]
    flops = 2 * count * cot.shape[1] * size * size
    return call(grads_kernel, outs, scalars, (*acts, cot), scratch, flops, 16 * MIB)


def tie(*values):
    return lax.optimization_barrier(values)


def near(block, axis):
    return shift(block, axis, -1), shift(block, axis, 1)


def far(following, previous, axis):
    half = following.shape[0] // 2
    top = shift(previous[:half], axis, 1)
    bottom = shift(following[half:], axis, -1)
    return top, bottom


def merge(up, down, got):
    from_before, from_after = got
    half = up.shape[0] // 2
    up = jnp.concatenate([up[:half] + from_before, up[half:]], axis=0)
    down = jnp.concatenate([down[:half], down[half:] + from_after], axis=0)
    return up, down


def local(acts, frozen, delta_tiles, delta_index, delta_count, cotangent):
    x, zl, core, y, zh = (lax.axis_index(a) for a in AXES)
    tokens, width = acts.shape
    per_owner, size = delta_tiles.shape[1], delta_tiles.shape[2]
    half_width = width // 2
    step = half_width // CHUNKS
    scaling = 1.0 / math.sqrt(tokens * RING * 4)
    where = jnp.stack([x, zl, core, zh, y]).astype(jnp.int32)
    own_is_b = zh == zl

    left, right = cotangent[:, :half_width], cotangent[:, half_width:]
    keep = jnp.where(core == 0, left, right)
    give = jnp.where(core == 0, right, left)

    def along_z(block):
        part_0 = lax.ppermute(block, ("zl", "zh"), [(0, 2), (1, 0), (2, 3), (3, 1)])
        part_1 = lax.ppermute(block, ("zl", "zh"), [(1, 2), (2, 1)])
        return part_0, part_1

    def parts(block, pair):
        return pair[0], jnp.where(own_is_b, block, pair[1])

    live = jnp.arange(per_owner, dtype=jnp.int32) < delta_count[0, 0]
    info = jnp.concatenate([delta_index[0], live[:, None].astype(jnp.int32)], axis=1)
    info = jnp.pad(info[:, None, :], ((0, 0), (0, EXTRA - 1), (0, size - 3)))
    mine = jnp.concatenate([delta_tiles[0] * live[:, None, None].astype(jnp.bfloat16), info.astype(jnp.bfloat16)], axis=1)

    frozen_0, frozen_1 = frozen[:, :step], frozen[:, step:]
    got_z = along_z(frozen_0)
    next_1, prev_1 = near(frozen_1, "x")
    cot_rows = jnp.concatenate([keep, swap(give, "core")], axis=0)
    other_mine = swap(mine, "zh")
    acts, frozen_0, got_z, mine, other_mine, cot_rows, next_1, prev_1 = tie(
        acts, frozen_0, got_z, mine, other_mine, cot_rows, next_1, prev_1
    )

    tiles = lax.all_gather(jnp.concatenate([mine, other_mine], axis=0), ("x", "zl", "core"), axis=0, tiled=True)
    cot_next, cot_prev = near(cot_rows, "y")
    acts_other = swap(acts, "zh")
    wide_1 = jnp.stack([frozen_1, next_1, jnp.concatenate(far(next_1, prev_1, "x"), axis=0), prev_1])
    got_1 = along_z(wide_1)
    cot_far = jnp.concatenate(far(cot_next, cot_prev, "y"), axis=0)
    cot_rows, cot_next, cot_far, cot_prev, acts, acts_other, frozen_0, got_z = tie(
        cot_rows, cot_next, cot_far, cot_prev, acts, acts_other, frozen_0, got_z
    )

    piece_0 = jnp.concatenate(parts(frozen_0, got_z), axis=0)
    next_0, prev_0 = near(piece_0, "x")
    swapped = swap(jnp.stack([acts, acts_other]), "core")
    cot = jnp.stack([cot_rows, cot_next, cot_far, cot_prev])
    next_0, prev_0, swapped, cot = tie(next_0, prev_0, swapped, cot)
    far_0 = far(next_0, prev_0, "x")
    codes = slot_codes(where, tiles[:, size, :3].astype(jnp.int32))
    slots = codes.shape[0]
    acts_all = (acts, acts_other, swapped)
    scalars = (where, codes)
    own_grads, other_grads = slot_grads(scalars, acts_all, cot, slots // 2, size)
    own_grads, other_grads, far_0, got_1, acts_all, cot = tie(own_grads, other_grads, far_0, got_1, acts_all, cot)

    blocks_0 = (piece_0, next_0, *far_0, prev_0)
    blocks_1 = (wide_1, *got_1)
    swapped_grads = swap(other_grads, "core")
    mine_out, up, far_top, far_bottom, down = forward(scalars, tiles, acts_all, blocks_0, blocks_1, step)
    mine_out, up, far_top, far_bottom, down, own_grads, swapped_grads, cot = tie(
        mine_out, up, far_top, far_bottom, down, own_grads, swapped_grads, cot
    )

    def slab(k):
        place = ((x + k) % RING) * (slots // 8)
        return lax.dynamic_slice_in_dim(own_grads, place, slots // 8, 0) + lax.dynamic_slice_in_dim(
            swapped_grads, place, slots // 8, 0
        )

    got = shift(far_top, "y", 1), shift(far_bottom, "y", -1)
    eighth = slots // 16
    far_slab = slab(2)
    got_g = shift(far_slab[:eighth], "x", 1), shift(far_slab[eighth:], "x", -1)
    keep, give = backward(scalars, tiles, cot, blocks_0, blocks_1, width)
    keep, give, got, got_g, up, down, own_grads, swapped_grads = tie(
        keep, give, got, got_g, up, down, own_grads, swapped_grads
    )

    given = swap(give, "core")
    up, down = merge(up, down, got)
    up_g, down_g = merge(slab(1), slab(3), got_g)
    keep, given, up, down, up_g, down_g = tie(keep, given, up, down, up_g, down_g)
    back_own, back_other = keep[0] + given[0], keep[1] + given[1]
    back_got = swap(back_other, "zh")
    got = shift(up, "y", 1), shift(down, "y", -1)
    got_g = shift(up_g, "x", 1), shift(down_g, "x", -1)

    grads = slab(0) + got_g[0] + got_g[1]
    grads_zl = grads.reshape(2, -1, size, size)
    grads = lax.dynamic_index_in_dim(grads_zl, zl, 0, keepdims=False) + swap(
        lax.dynamic_index_in_dim(grads_zl, 1 - zl, 0, keepdims=False), "zl"
    )
    grads = grads[:per_owner] + swap(grads[per_owner:], "zh")
    delta_grad = (grads * scaling * live[:, None, None].astype(jnp.float32))[None]

    mine_out = (mine_out + got[0] + got[1]).astype(jnp.bfloat16)
    kept, got = mine_out[:tokens], swap(mine_out[tokens:], "core")
    output = jnp.concatenate([jnp.where(core == 0, kept, got), jnp.where(core == 0, got, kept)], axis=1)
    grad_input = (back_own + back_got).astype(jnp.bfloat16)
    return output, grad_input, delta_grad


def solution(mesh):
    fine = Mesh(mesh.devices.reshape(4, 2, 2, 4, 2), AXES)
    rows, cols = ("x", "zl", "core"), ("y", "zh")
    return jax.shard_map(
        local,
        mesh=fine,
        in_specs=(
            P(rows, cols),
            P(cols, rows),
            P(cols, rows, None, None),
            P(cols, rows, None),
            P(cols, rows),
            P(rows, cols),
        ),
        out_specs=(P(rows, cols), P(rows, cols), P(cols, rows, None, None)),
        check_vma=False,
    )
```

```python
import functools
import math

import jax
import jax.numpy as jnp
from jax import lax
from jax.experimental import pallas as pl
from jax.experimental.pallas import tpu as pltpu
from jax.sharding import Mesh, PartitionSpec as P

AXES = ("x", "zl", "core", "y", "zh")
RING = 4
CHUNKS = 2
EXTRA = 16
COST = 1000
VMEM_LIMIT = 60 * 1024 * 1024


def shift(value, axis, step):
    return lax.ppermute(value, axis, [(i, (i + step) % RING) for i in range(RING)])


def swap(value, axis):
    return lax.ppermute(value, axis, [(0, 1), (1, 0)])


def dot(a, b):
    return jnp.dot(a, b, preferred_element_type=jnp.float32)


def dot_t(a, b):
    return lax.dot_general(a, b, (((1,), (1,)), ((), ())), preferred_element_type=jnp.float32)


def slot_codes(where, info):
    x, zl, core, zh, _ = (where[i] for i in range(5))
    row, col, live = info[:, 0], info[:, 1], info[:, 2]
    slot = jnp.arange(info.shape[0], dtype=jnp.int32)
    slice_zh = zh ^ ((slot >> 2) & 1)
    here = (live > 0) & (((col >> 3) & 1) == zh) & (((col >> 2) & 1) == core)
    ring = ((col >> 4) + RING - x) & 3
    part = 1 - (slice_zh ^ zl)
    code = (part << 8) | (row << 5) | (((col >> 1) & 1) << 4) | (ring << 2) | (col & 1)
    return jnp.where(here, code, -1)


def slot_place(code):
    return code >> 8, (code >> 5) & 7, (code >> 4) & 1, (code >> 2) & 3, code & 1


def block_at(index, size):
    return pl.ds(pl.multiple_of(index * size, size), size)


def start_all(copies, sems):
    started = []
    for i, (source, target, *choice) in enumerate(copies):
        copy = pltpu.make_async_copy(source, target, sems.at[i])
        if choice:
            flag, instead = choice
            pl.when(flag)(pltpu.make_async_copy(instead, target, sems.at[i]).start)
            pl.when(jnp.logical_not(flag))(copy.start)
        else:
            copy.start()
        started.append(copy)
    return started


def each_slot(codes_ref, tiles_ref, body):
    def one(slot, carry):
        code = codes_ref[slot]

        @pl.when(code >= 0)
        def _():
            body(slot_place(code), tiles_ref[slot])

        return carry

    lax.fori_loop(0, tiles_ref.shape[0], one, 0)


def block_copies(where_ref, refs, part, rows, target_of):
    same = where_ref[1] == where_ref[3]
    first, length = rows
    copies = []
    for ring in range(RING):
        target = target_of(ring)
        if len(refs) == 6:
            sent, got = (
                ref.at[ring % 2, pl.ds(first, length)] for ref in (refs[ring // 2], refs[2 + ring // 2 * 2 + part])
            )
            copies.append((got, target, same, sent) if part == 1 else (got, target))
        elif ring == 2:
            copies.append((refs[2 + part].at[pl.ds(first, length)], target))
        else:
            depth = refs[0].shape[0] // 2
            copies.append((refs[(0, 1, None, 4)[ring]].at[pl.ds(part * depth + first, length)], target))
    return copies


def clear(ref):
    def one(i, carry):
        ref[i] = jnp.zeros(ref.shape[1:], ref.dtype)
        return carry

    lax.fori_loop(0, ref.shape[0], one, 0)


def acts_copies(where_ref, refs, acts):
    own = 1 - where_ref[3] ^ where_ref[1]
    acts_ref, other_ref, swapped_ref = refs
    tokens, depth = acts_ref.shape
    rows = pl.ds(0, tokens), pl.ds(tokens, tokens)
    cols = [pl.ds(pl.multiple_of(part * depth, depth), depth) for part in (own, 1 - own)]
    return [
        (acts_ref, acts.at[rows[0], cols[0]]),
        (other_ref, acts.at[rows[0], cols[1]]),
        (swapped_ref.at[0], acts.at[rows[1], cols[0]]),
        (swapped_ref.at[1], acts.at[rows[1], cols[1]]),
    ]


def slot_forward_kernel(where_ref, codes_ref, tiles_ref, *refs):
    acts_refs, (out_ref, acts, tiles, sums, sems) = refs[:3], refs[3:]
    size = tiles.shape[2]
    rows = acts.shape[1] // size // 2
    per_chunk = sums.shape[2] // size // CHUNKS
    started = start_all([*acts_copies(where_ref, acts_refs, acts), (tiles_ref.at[:, pl.ds(0, size)], tiles)], sems)
    clear(sums)
    for copy in started:
        copy.wait()

    def add(place, tile):
        part, row, chunk, ring, col = place
        r, c = block_at(part * rows + row, size), block_at(chunk * per_chunk + col, size)
        sums[ring, :, c] += dot(acts[:, r], tile)

    each_slot(codes_ref, tiles, add)
    for copy in start_all([(sums, out_ref)], sems):
        copy.wait()


def slot_backward_kernel(where_ref, codes_ref, tiles_ref, cot_ref, *refs):
    acts_refs, (back_ref, own_ref, other_ref, acts, cot, tiles, sums, grads, sems) = refs[:3], refs[3:]
    size = tiles.shape[2]
    half = own_ref.shape[0]
    rows = acts.shape[1] // size // 2
    x, core, y = where_ref[0], where_ref[2], where_ref[4]
    copies = [*acts_copies(where_ref, acts_refs, acts), (cot_ref, cot), (tiles_ref.at[:, pl.ds(0, size)], tiles)]
    started = start_all(copies, sems)
    clear(sums)
    for copy in started:
        copy.wait()

    def fill(owner_core, first):
        def one(i, carry):
            slot = ((i >> 4) << 5) + (owner_core << 4) + (i & 15)
            code = codes_ref[slot]

            @pl.when(code >= 0)
            def _():
                part, row, chunk, ring, col = slot_place(code)
                cots = cot[(ring + x + RING - y) & 3, :, block_at(2 * chunk + col, size)]
                sums[part, :, block_at(row, size)] += dot_t(cots, tiles[slot])
                grads[first + i] = lax.dot_general(
                    acts[:, block_at(part * rows + row, size)],
                    cots,
                    (((0,), (0,)), ((), ())),
                    preferred_element_type=jnp.float32,
                )

            @pl.when(code < 0)
            def _():
                grads[first + i] = jnp.zeros((size, size), jnp.float32)

            return carry

        lax.fori_loop(0, half, one, 0)

    fill(1 - core, half)
    other_out = pltpu.make_async_copy(grads.at[pl.ds(half, half)], other_ref, sems.at[0])
    other_out.start()
    fill(core, 0)
    last = [
        pltpu.make_async_copy(grads.at[pl.ds(0, half)], own_ref, sems.at[1]),
        pltpu.make_async_copy(sums, back_ref, sems.at[2]),
    ]
    for copy in last:
        copy.start()
    for copy in (other_out, *last):
        copy.wait()


def forward_kernel(where_ref, delta_ref, *refs):
    acts_refs, blocks_0, blocks_1, rest = refs[:3], refs[3:8], refs[8:14], refs[14:]
    (mine_ref, up_ref, far_top_ref, far_bottom_ref, down_ref), (acts, blocks, sums, sems, out_sems) = rest[:5], rest[5:]
    x, y = where_ref[0], where_ref[4]
    step = sums.shape[2] // CHUNKS
    depth = blocks.shape[1] // 2
    half = acts.shape[0] // 2

    rings = [[(delta_ref.at[ring], sums.at[ring])] for ring in range(RING)]
    for chunk, chunk_refs in enumerate((blocks_0, blocks_1)):
        for part in range(2):

            def target(ring, chunk=chunk, part=part):
                return blocks.at[ring, pl.ds(part * depth, depth), pl.ds(chunk * step, step)]

            for ring, copy in enumerate(block_copies(where_ref, chunk_refs, part, (0, depth), target)):
                rings[ring].append(copy)
    each = len(rings[0])
    started = start_all(acts_copies(where_ref, acts_refs, acts) + rings[0], sems)
    for ring in range(RING):
        for copy in started:
            copy.wait()
        if ring + 1 < RING:
            started = start_all(rings[ring + 1], sems.at[pl.ds((ring % 2 + 1) * 9, each)])
        sums[ring] += dot(acts[...], blocks[ring])
        place = (x + RING + ring - y) & 3
        for k, ref in ((0, mine_ref), (1, up_ref), (3, down_ref)):
            pl.when(place == k)(pltpu.make_async_copy(sums.at[ring], ref, out_sems.at[k]).start)
        for i, ref in enumerate((far_top_ref, far_bottom_ref)):
            source = sums.at[ring, pl.ds(i * half, half)]
            pl.when(place == 2)(pltpu.make_async_copy(source, ref, out_sems.at[2 + 2 * i]).start)
    for k, ref in ((0, mine_ref), (1, up_ref), (3, down_ref), (2, far_top_ref), (4, far_bottom_ref)):
        pltpu.make_async_copy(sums.at[0, pl.ds(0, ref.shape[0])], ref, out_sems.at[k]).wait()


def backward_kernel(own, where_ref, delta_ref, cot_ref, *refs):
    blocks_0, blocks_1, rest = refs[:5], refs[5:11], refs[11:]
    (keep_ref, give_ref), (cot, blocks, sums, sems, out_sems) = rest[:2], rest[2:]
    x, zl, zh, y = where_ref[0], where_ref[1], where_ref[3], where_ref[4]
    mine = 1 - zh ^ zl if own else zh ^ zl
    step = cot_ref.shape[2] // CHUNKS
    tokens = keep_ref.shape[0]
    half = blocks.shape[0] // 2
    each = CHUNKS * RING

    def columns(n):
        return pl.ds(n * step, step)

    cots = []
    for chunk in range(CHUNKS):
        for ring in range(RING):
            source = cot_ref.at[(x + ring + RING - y) & 3, :, pl.ds(chunk * step, step)]
            cots.append((source, cot.at[:, columns(chunk * RING + ring)]))

    def start_piece(i):
        rows = pl.ds(i * half, half)
        for part in range(2):

            @pl.when(mine == part)
            def _(part=part):
                copies = []
                for chunk, chunk_refs in enumerate((blocks_0, blocks_1)):

                    def target(ring, chunk=chunk):
                        return blocks.at[rows, columns(chunk * RING + ring)]

                    copies += block_copies(where_ref, chunk_refs, part, (i * half, half), target)
                start_all(copies, sems.at[pl.ds(each * (1 + i), each)])

        waits = [pltpu.make_async_copy(delta_ref.at[mine, :, rows], sums.at[:, rows], out_sems.at[i])]
        waits[0].start()
        for n in range(each):
            target = blocks.at[rows, columns(n)]
            waits.append(pltpu.make_async_copy(target, target, sems.at[each * (1 + i) + n]))
        return waits

    started = start_all(cots, sems) + start_piece(0)
    for i in range(2):
        for copy in started:
            copy.wait()
        if i == 0:
            started = start_piece(1)
        rows = slice(i * half, (i + 1) * half)
        sums[:, rows] += dot_t(cot[...], blocks[rows])
    out = start_all([(sums.at[pl.ds(tokens, tokens)], give_ref), (sums.at[pl.ds(0, tokens)], keep_ref)], out_sems)
    for copy in out:
        copy.wait()


def floats(*shape):
    return jax.ShapeDtypeStruct(shape, jnp.float32)


def call(kernel, outs, scalars, operands, scratch, flops, moved):
    in_specs = [pl.BlockSpec(memory_space=pltpu.SMEM)] * len(scalars)
    in_specs += [pl.BlockSpec(memory_space=pl.ANY)] * len(operands)
    return pl.pallas_call(
        kernel,
        out_shape=outs,
        in_specs=in_specs,
        out_specs=[pl.BlockSpec(memory_space=pl.ANY)] * len(outs),
        scratch_shapes=scratch,
        compiler_params=pltpu.CompilerParams(vmem_limit_bytes=VMEM_LIMIT),
        cost_estimate=pl.CostEstimate(flops=flops // COST, bytes_accessed=moved // COST, transcendentals=0),
    )(*scalars, *operands)


MIB = 1024 * 1024


def slot_forward(scalars, tiles, acts, width):
    rows, depth = 2 * acts[0].shape[0], acts[0].shape[1]
    count, size = tiles.shape[0], tiles.shape[2]
    scratch = [
        pltpu.VMEM((rows, 2 * depth), jnp.bfloat16),
        pltpu.VMEM((count, size, size), jnp.bfloat16),
        pltpu.VMEM((RING, rows, width), jnp.float32),
        pltpu.SemaphoreType.DMA((5,)),
    ]
    flops = count * rows * size * size
    return call(slot_forward_kernel, [floats(RING, rows, width)], scalars, (tiles, *acts), scratch, flops, 16 * MIB)[0]


def slot_backward(scalars, tiles, cot, acts):
    rows, depth = 2 * acts[0].shape[0], acts[0].shape[1]
    count, size = tiles.shape[0], tiles.shape[2]
    outs = [floats(2, rows, depth)] + [floats(count // 2, size, size)] * 2
    scratch = [
        pltpu.VMEM((rows, 2 * depth), jnp.bfloat16),
        pltpu.VMEM(cot.shape, jnp.bfloat16),
        pltpu.VMEM((count, size, size), jnp.bfloat16),
        pltpu.VMEM((2, rows, depth), jnp.float32),
        pltpu.VMEM((count, size, size), jnp.float32),
        pltpu.SemaphoreType.DMA((6,)),
    ]
    flops = 2 * count * rows * size * size
    return call(slot_backward_kernel, outs, scalars, (tiles, cot, *acts), scratch, flops, 24 * MIB)


def forward(where, delta, acts, blocks_0, blocks_1):
    rows, depth = 2 * acts[0].shape[0], acts[0].shape[1]
    width = delta.shape[2]
    outs = [floats(rows, width)] * 2 + [floats(rows // 2, width)] * 2 + [floats(rows, width)]
    scratch = [
        pltpu.VMEM((rows, 2 * depth), jnp.bfloat16),
        pltpu.VMEM((RING, 2 * depth, width), jnp.bfloat16),
        pltpu.VMEM((RING, rows, width), jnp.float32),
        pltpu.SemaphoreType.DMA((27,)),
        pltpu.SemaphoreType.DMA((5,)),
    ]
    flops = 4 * RING * rows * depth * width
    operands = (delta, *acts, *blocks_0, *blocks_1)
    return call(forward_kernel, outs, (where,), operands, scratch, flops, 24 * MIB)


def backward(own, where, delta, cot, blocks_0, blocks_1):
    _, rows, depth = delta.shape
    width = RING * cot.shape[2]
    outs = [floats(rows // 2, depth)] * 2
    scratch = [
        pltpu.VMEM((rows, width), jnp.bfloat16),
        pltpu.VMEM((depth, width), jnp.bfloat16),
        pltpu.VMEM((rows, depth), jnp.float32),
        pltpu.SemaphoreType.DMA((3 * CHUNKS * RING,)),
        pltpu.SemaphoreType.DMA((2,)),
    ]
    flops = 2 * rows * depth * width
    operands = (delta, cot, *blocks_0, *blocks_1)
    return call(functools.partial(backward_kernel, own), outs, (where,), operands, scratch, flops, 16 * MIB)


def tie(*values):
    return lax.optimization_barrier(values)


def near(block, axis):
    return shift(block, axis, -1), shift(block, axis, 1)


def far(following, previous, axis):
    half = following.shape[0] // 2
    top = shift(previous[:half], axis, 1)
    bottom = shift(following[half:], axis, -1)
    return top, bottom


def merge(up, down, got):
    from_before, from_after = got
    half = up.shape[0] // 2
    up = up.at[:half].add(from_before)
    down = down.at[half:].add(from_after)
    return up, down


def local(acts, frozen, delta_tiles, delta_index, delta_count, cotangent):
    x, zl, core, y, zh = (lax.axis_index(a) for a in AXES)
    tokens, width = acts.shape
    per_owner, size = delta_tiles.shape[1], delta_tiles.shape[2]
    half_width = width // 2
    step = half_width // CHUNKS
    scaling = 1.0 / math.sqrt(tokens * RING * 4)
    where = jnp.stack([x, zl, core, zh, y]).astype(jnp.int32)
    own_is_b = zh == zl

    left, right = cotangent[:, :half_width], cotangent[:, half_width:]
    keep = jnp.where(core == 0, left, right)
    give = jnp.where(core == 0, right, left)

    def along_z(block):
        part_0 = lax.ppermute(block, ("zl", "zh"), [(0, 2), (1, 0), (2, 3), (3, 1)])
        part_1 = lax.ppermute(block, ("zl", "zh"), [(1, 2), (2, 1)])
        return part_0, part_1

    def parts(block, pair):
        return pair[0], jnp.where(own_is_b, block, pair[1])

    live = jnp.arange(per_owner, dtype=jnp.int32) < delta_count[0, 0]
    info = jnp.concatenate([delta_index[0], live[:, None].astype(jnp.int32)], axis=1)
    info = jnp.pad(info[:, None, :], ((0, 0), (0, EXTRA - 1), (0, size - 3)))
    mine = jnp.concatenate([delta_tiles[0] * live[:, None, None].astype(jnp.bfloat16), info.astype(jnp.bfloat16)], axis=1)

    frozen_0, frozen_1 = frozen[:, :step], frozen[:, step:]
    got_z = along_z(frozen_0)
    next_1, prev_1 = near(frozen_1, "x")
    far_1 = far(next_1, prev_1, "x")
    cot_rows = jnp.concatenate([keep, swap(give, "core")], axis=0)
    pair = jnp.concatenate([mine, swap(mine, "zh")], axis=0)
    other_pair = swap(pair, "zl")
    acts, frozen_0, got_z, pair, other_pair, cot_rows, frozen_1, next_1, far_1, prev_1 = tie(
        acts, frozen_0, got_z, pair, other_pair, cot_rows, frozen_1, next_1, far_1, prev_1
    )

    quad = jnp.concatenate([jnp.where(zl == 0, pair, other_pair), jnp.where(zl == 0, other_pair, pair)], axis=0)
    tiles = lax.all_gather(quad, ("x", "core"), axis=0, tiled=True)
    first_1 = jnp.stack([frozen_1, next_1])
    second_1 = jnp.stack([jnp.concatenate(far_1, axis=0), prev_1])
    got_first = along_z(first_1)
    acts_other = swap(acts, "zh")
    cot_next, cot_prev = near(cot_rows, "y")
    cot_far = jnp.concatenate(far(cot_next, cot_prev, "y"), axis=0)
    cot_rows, cot_next, cot_far, cot_prev, frozen_0, got_z, got_first, second_1 = tie(
        cot_rows, cot_next, cot_far, cot_prev, frozen_0, got_z, got_first, second_1
    )

    piece_0 = jnp.concatenate(parts(frozen_0, got_z), axis=0)
    next_0, prev_0 = near(piece_0, "x")
    got_second = along_z(second_1)
    swapped = swap(jnp.stack([acts, acts_other]), "core")
    cot = jnp.stack([cot_rows, cot_next, cot_far, cot_prev])
    codes = slot_codes(where, tiles[:, size, :3].astype(jnp.int32))
    slots = codes.shape[0]
    acts_all = (acts, acts_other, swapped)
    scalars = (where, codes)
    delta_back, own_grads, other_grads = slot_backward(scalars, tiles, cot, acts_all)
    next_0, prev_0, got_second, delta_back, own_grads, other_grads, cot, acts_all = tie(
        next_0, prev_0, got_second, delta_back, own_grads, other_grads, cot, acts_all
    )
    far_0 = far(next_0, prev_0, "x")
    swapped_grads = swap(other_grads, "core")
    delta_out = slot_forward(scalars, tiles, acts_all, half_width)
    delta_out, own_grads, swapped_grads, far_0, acts_all = tie(delta_out, own_grads, swapped_grads, far_0, acts_all)

    def slab(k):
        place = ((x + k) % RING) * (slots // 8)
        return lax.dynamic_slice_in_dim(own_grads, place, slots // 8, 0) + lax.dynamic_slice_in_dim(
            swapped_grads, place, slots // 8, 0
        )

    eighth = slots // 16
    blocks_0 = (piece_0, next_0, *far_0, prev_0)
    blocks_1 = (first_1, second_1, *got_first, *got_second)
    other_keep, other_give = backward(False, where, delta_back, cot, blocks_0, blocks_1)
    other_keep, other_give, delta_out, own_grads, swapped_grads = tie(
        other_keep, other_give, delta_out, own_grads, swapped_grads
    )

    other_given = swap(other_give, "core")
    far_slab = slab(2)
    other_keep, other_given, delta_out, far_slab = tie(other_keep, other_given, delta_out, far_slab)
    back_got = swap(other_keep + other_given, "zh")
    got_g = shift(far_slab[:eighth], "x", 1), shift(far_slab[eighth:], "x", -1)
    mine_out, up, far_top, far_bottom, down = forward(where, delta_out, acts_all, blocks_0, blocks_1)
    mine_out, up, far_top, far_bottom, down, cot, got_g = tie(mine_out, up, far_top, far_bottom, down, cot, got_g)

    got = shift(far_top, "y", 1), shift(far_bottom, "y", -1)
    up_g, down_g = merge(slab(1), slab(3), got_g)
    got_g = shift(up_g, "x", 1), shift(down_g, "x", -1)
    own_keep, own_give = backward(True, where, delta_back, cot, blocks_0, blocks_1)
    own_keep, own_give, got, up, down, back_got = tie(own_keep, own_give, got, up, down, back_got)

    up, down = merge(up, down, got)
    got = shift(up, "y", 1), shift(down, "y", -1)
    back_own = own_keep + swap(own_give, "core")

    grads = slab(0) + got_g[0] + got_g[1]
    grads_zl = grads.reshape(2, -1, size, size)
    grads = lax.dynamic_index_in_dim(grads_zl, zl, 0, keepdims=False) + swap(
        lax.dynamic_index_in_dim(grads_zl, 1 - zl, 0, keepdims=False), "zl"
    )
    grads = grads[:per_owner] + swap(grads[per_owner:], "zh")
    delta_grad = (grads * scaling * live[:, None, None].astype(jnp.float32))[None]

    mine_out = (mine_out + got[0] + got[1]).astype(jnp.bfloat16)
    kept, got = mine_out[:tokens], swap(mine_out[tokens:], "core")
    output = jnp.concatenate([jnp.where(core == 0, kept, got), jnp.where(core == 0, got, kept)], axis=1)
    grad_input = (back_own + back_got).astype(jnp.bfloat16)
    return output, grad_input, delta_grad


def solution(mesh):
    fine = Mesh(mesh.devices.reshape(4, 2, 2, 4, 2), AXES)
    rows, cols = ("x", "zl", "core"), ("y", "zh")
    return jax.shard_map(
        local,
        mesh=fine,
        in_specs=(
            P(rows, cols),
            P(cols, rows),
            P(cols, rows, None, None),
            P(cols, rows, None),
            P(cols, rows),
            P(rows, cols),
        ),
        out_specs=(P(rows, cols), P(rows, cols), P(cols, rows, None, None)),
        check_vma=False,
    )
```

```python
import functools
import math

import jax
import jax.numpy as jnp
from jax import lax
from jax.experimental import pallas as pl
from jax.experimental.pallas import tpu as pltpu
from jax.sharding import Mesh, PartitionSpec as P

AXES = ("x", "zl", "core", "y", "zh")
RING = 4
CHUNKS = 2
EXTRA = 16
COST = 1000
VMEM_LIMIT = 60 * 1024 * 1024


def shift(value, axis, step):
    return lax.ppermute(value, axis, [(i, (i + step) % RING) for i in range(RING)])


def swap(value, axis):
    return lax.ppermute(value, axis, [(0, 1), (1, 0)])


def dot(a, b):
    return jnp.dot(a, b, preferred_element_type=jnp.float32)


def dot_t(a, b):
    return lax.dot_general(a, b, (((1,), (1,)), ((), ())), preferred_element_type=jnp.float32)


def slot_codes(where, info):
    x, zl, core, zh, _ = (where[i] for i in range(5))
    row, col, live = info[:, 0], info[:, 1], info[:, 2]
    slot = jnp.arange(info.shape[0], dtype=jnp.int32)
    slice_zh = zh ^ ((slot >> 2) & 1)
    here = (live > 0) & (((col >> 3) & 1) == zh) & (((col >> 2) & 1) == core)
    ring = ((col >> 4) + RING - x) & 3
    part = 1 - (slice_zh ^ zl)
    code = (part << 8) | (row << 5) | (((col >> 1) & 1) << 4) | (ring << 2) | (col & 1)
    return jnp.where(here, code, -1)


def slot_place(code):
    return code >> 8, (code >> 5) & 7, (code >> 4) & 1, (code >> 2) & 3, code & 1


def block_at(index, size):
    return pl.ds(pl.multiple_of(index * size, size), size)


def start_all(copies, sems):
    started = []
    for i, (source, target, *choice) in enumerate(copies):
        copy = pltpu.make_async_copy(source, target, sems.at[i])
        if choice:
            flag, instead = choice
            pl.when(flag)(pltpu.make_async_copy(instead, target, sems.at[i]).start)
            pl.when(jnp.logical_not(flag))(copy.start)
        else:
            copy.start()
        started.append(copy)
    return started


def each_slot(codes_ref, tiles_ref, body):
    def one(slot, carry):
        code = codes_ref[slot]

        @pl.when(code >= 0)
        def _():
            body(slot_place(code), tiles_ref[slot])

        return carry

    lax.fori_loop(0, tiles_ref.shape[0], one, 0)


def block_copies(where_ref, refs, part, rows, target_of):
    same = where_ref[1] == where_ref[3]
    first, length = rows
    copies = []
    for ring in range(RING):
        target = target_of(ring)
        if len(refs) == 9:
            piece = (0, 1, 1, 2)[ring]
            sent, got = (
                (ref.at[ring - 1] if piece == 1 else ref).at[pl.ds(first, length)]
                for ref in (refs[piece], refs[3 + 2 * piece + part])
            )
            copies.append((got, target, same, sent) if part == 1 else (got, target))
        elif ring == 2:
            copies.append((refs[2 + part].at[pl.ds(first, length)], target))
        else:
            depth = refs[0].shape[0] // 2
            copies.append((refs[(0, 1, None, 4)[ring]].at[pl.ds(part * depth + first, length)], target))
    return copies


def clear(ref):
    def one(i, carry):
        ref[i] = jnp.zeros(ref.shape[1:], ref.dtype)
        return carry

    lax.fori_loop(0, ref.shape[0], one, 0)


def acts_copies(where_ref, refs, acts):
    own = 1 - where_ref[3] ^ where_ref[1]
    acts_ref, other_ref, swapped_ref = refs
    tokens, depth = acts_ref.shape
    rows = pl.ds(0, tokens), pl.ds(tokens, tokens)
    cols = [pl.ds(pl.multiple_of(part * depth, depth), depth) for part in (own, 1 - own)]
    return [
        (acts_ref, acts.at[rows[0], cols[0]]),
        (other_ref, acts.at[rows[0], cols[1]]),
        (swapped_ref.at[0], acts.at[rows[1], cols[0]]),
        (swapped_ref.at[1], acts.at[rows[1], cols[1]]),
    ]


def slot_forward_kernel(where_ref, codes_ref, tiles_ref, *refs):
    acts_refs, (out_ref, acts, tiles, sums, sems) = refs[:3], refs[3:]
    size = tiles.shape[2]
    rows = acts.shape[1] // size // 2
    per_chunk = sums.shape[2] // size // CHUNKS
    started = start_all([*acts_copies(where_ref, acts_refs, acts), (tiles_ref.at[:, pl.ds(0, size)], tiles)], sems)
    clear(sums)
    for copy in started:
        copy.wait()

    def add(place, tile):
        part, row, chunk, ring, col = place
        r, c = block_at(part * rows + row, size), block_at(chunk * per_chunk + col, size)
        sums[ring, :, c] += dot(acts[:, r], tile)

    each_slot(codes_ref, tiles, add)
    for copy in start_all([(sums, out_ref)], sems):
        copy.wait()


def slot_backward_kernel(where_ref, codes_ref, tiles_ref, cot_ref, *refs):
    acts_refs, (back_ref, own_ref, other_ref, acts, cot, tiles, sums, grads, sems) = refs[:3], refs[3:]
    size = tiles.shape[2]
    half = own_ref.shape[0]
    rows = acts.shape[1] // size // 2
    x, core, y = where_ref[0], where_ref[2], where_ref[4]
    copies = [*acts_copies(where_ref, acts_refs, acts), (cot_ref, cot), (tiles_ref.at[:, pl.ds(0, size)], tiles)]
    started = start_all(copies, sems)
    clear(sums)
    for copy in started:
        copy.wait()

    def fill(owner_core, first):
        def one(i, carry):
            slot = ((i >> 4) << 5) + (owner_core << 4) + (i & 15)
            code = codes_ref[slot]

            @pl.when(code >= 0)
            def _():
                part, row, chunk, ring, col = slot_place(code)
                cots = cot[(ring + x + RING - y) & 3, :, block_at(2 * chunk + col, size)]
                sums[part, :, block_at(row, size)] += dot_t(cots, tiles[slot])
                grads[first + i] = lax.dot_general(
                    acts[:, block_at(part * rows + row, size)],
                    cots,
                    (((0,), (0,)), ((), ())),
                    preferred_element_type=jnp.float32,
                )

            @pl.when(code < 0)
            def _():
                grads[first + i] = jnp.zeros((size, size), jnp.float32)

            return carry

        lax.fori_loop(0, half, one, 0)

    fill(1 - core, half)
    other_out = pltpu.make_async_copy(grads.at[pl.ds(half, half)], other_ref, sems.at[0])
    other_out.start()
    fill(core, 0)
    last = [
        pltpu.make_async_copy(grads.at[pl.ds(0, half)], own_ref, sems.at[1]),
        pltpu.make_async_copy(sums, back_ref, sems.at[2]),
    ]
    for copy in last:
        copy.start()
    for copy in (other_out, *last):
        copy.wait()


def forward_kernel(where_ref, delta_ref, *refs):
    acts_refs, blocks_0, blocks_1, rest = refs[:3], refs[3:8], refs[8:17], refs[17:]
    (mine_ref, up_ref, far_top_ref, far_bottom_ref, down_ref), (acts, blocks, sums, sems, out_sems) = rest[:5], rest[5:]
    x, y = where_ref[0], where_ref[4]
    step = sums.shape[2] // CHUNKS
    depth = blocks.shape[1] // 2
    half = acts.shape[0] // 2

    rings = [[(delta_ref.at[ring], sums.at[ring])] for ring in range(RING)]
    for chunk, chunk_refs in enumerate((blocks_0, blocks_1)):
        for part in range(2):

            def target(ring, chunk=chunk, part=part):
                return blocks.at[ring, pl.ds(part * depth, depth), pl.ds(chunk * step, step)]

            for ring, copy in enumerate(block_copies(where_ref, chunk_refs, part, (0, depth), target)):
                rings[ring].append(copy)
    each = len(rings[0])
    started = start_all(acts_copies(where_ref, acts_refs, acts) + rings[0], sems)
    for ring in range(RING):
        for copy in started:
            copy.wait()
        if ring + 1 < RING:
            started = start_all(rings[ring + 1], sems.at[pl.ds((ring % 2 + 1) * 9, each)])
        sums[ring] += dot(acts[...], blocks[ring])
        place = (x + RING + ring - y) & 3
        for k, ref in ((0, mine_ref), (1, up_ref), (3, down_ref)):
            pl.when(place == k)(pltpu.make_async_copy(sums.at[ring], ref, out_sems.at[k]).start)
        for i, ref in enumerate((far_top_ref, far_bottom_ref)):
            source = sums.at[ring, pl.ds(i * half, half)]
            pl.when(place == 2)(pltpu.make_async_copy(source, ref, out_sems.at[2 + 2 * i]).start)
    for k, ref in ((0, mine_ref), (1, up_ref), (3, down_ref), (2, far_top_ref), (4, far_bottom_ref)):
        pltpu.make_async_copy(sums.at[0, pl.ds(0, ref.shape[0])], ref, out_sems.at[k]).wait()


def backward_kernel(own, where_ref, delta_ref, cot_ref, *refs):
    blocks_0, blocks_1, rest = refs[:5], refs[5:14], refs[14:]
    (keep_ref, give_ref), (cot, blocks, sums, sems, out_sems) = rest[:2], rest[2:]
    x, zl, zh, y = where_ref[0], where_ref[1], where_ref[3], where_ref[4]
    mine = 1 - zh ^ zl if own else zh ^ zl
    step = cot_ref.shape[2] // CHUNKS
    tokens = keep_ref.shape[0]
    half = blocks.shape[0] // 2
    each = CHUNKS * RING

    def columns(n):
        return pl.ds(n * step, step)

    cots = []
    for chunk in range(CHUNKS):
        for ring in range(RING):
            source = cot_ref.at[(x + ring + RING - y) & 3, :, pl.ds(chunk * step, step)]
            cots.append((source, cot.at[:, columns(chunk * RING + ring)]))

    def start_piece(i):
        rows = pl.ds(i * half, half)
        for part in range(2):

            @pl.when(mine == part)
            def _(part=part):
                copies = []
                for chunk, chunk_refs in enumerate((blocks_0, blocks_1)):

                    def target(ring, chunk=chunk):
                        return blocks.at[rows, columns(chunk * RING + ring)]

                    copies += block_copies(where_ref, chunk_refs, part, (i * half, half), target)
                start_all(copies, sems.at[pl.ds(each * (1 + i), each)])

        waits = [pltpu.make_async_copy(delta_ref.at[mine, :, rows], sums.at[:, rows], out_sems.at[i])]
        waits[0].start()
        for n in range(each):
            target = blocks.at[rows, columns(n)]
            waits.append(pltpu.make_async_copy(target, target, sems.at[each * (1 + i) + n]))
        return waits

    started = start_all(cots, sems) + start_piece(0)
    for i in range(2):
        for copy in started:
            copy.wait()
        if i == 0:
            started = start_piece(1)
        rows = slice(i * half, (i + 1) * half)
        sums[:, rows] += dot_t(cot[...], blocks[rows])
    out = start_all([(sums.at[pl.ds(tokens, tokens)], give_ref), (sums.at[pl.ds(0, tokens)], keep_ref)], out_sems)
    for copy in out:
        copy.wait()


def floats(*shape):
    return jax.ShapeDtypeStruct(shape, jnp.float32)


def call(kernel, outs, scalars, operands, scratch, flops, moved):
    in_specs = [pl.BlockSpec(memory_space=pltpu.SMEM)] * len(scalars)
    in_specs += [pl.BlockSpec(memory_space=pl.ANY)] * len(operands)
    return pl.pallas_call(
        kernel,
        out_shape=outs,
        in_specs=in_specs,
        out_specs=[pl.BlockSpec(memory_space=pl.ANY)] * len(outs),
        scratch_shapes=scratch,
        compiler_params=pltpu.CompilerParams(vmem_limit_bytes=VMEM_LIMIT),
        cost_estimate=pl.CostEstimate(flops=flops // COST, bytes_accessed=moved // COST, transcendentals=0),
    )(*scalars, *operands)


MIB = 1024 * 1024


def slot_forward(scalars, tiles, acts, width):
    rows, depth = 2 * acts[0].shape[0], acts[0].shape[1]
    count, size = tiles.shape[0], tiles.shape[2]
    scratch = [
        pltpu.VMEM((rows, 2 * depth), jnp.bfloat16),
        pltpu.VMEM((count, size, size), jnp.bfloat16),
        pltpu.VMEM((RING, rows, width), jnp.float32),
        pltpu.SemaphoreType.DMA((5,)),
    ]
    flops = count * rows * size * size
    return call(slot_forward_kernel, [floats(RING, rows, width)], scalars, (tiles, *acts), scratch, flops, 16 * MIB)[0]


def slot_backward(scalars, tiles, cot, acts):
    rows, depth = 2 * acts[0].shape[0], acts[0].shape[1]
    count, size = tiles.shape[0], tiles.shape[2]
    outs = [floats(2, rows, depth)] + [floats(count // 2, size, size)] * 2
    scratch = [
        pltpu.VMEM((rows, 2 * depth), jnp.bfloat16),
        pltpu.VMEM(cot.shape, jnp.bfloat16),
        pltpu.VMEM((count, size, size), jnp.bfloat16),
        pltpu.VMEM((2, rows, depth), jnp.float32),
        pltpu.VMEM((count, size, size), jnp.float32),
        pltpu.SemaphoreType.DMA((6,)),
    ]
    flops = 2 * count * rows * size * size
    return call(slot_backward_kernel, outs, scalars, (tiles, cot, *acts), scratch, flops, 24 * MIB)


def forward(where, delta, acts, blocks_0, blocks_1):
    rows, depth = 2 * acts[0].shape[0], acts[0].shape[1]
    width = delta.shape[2]
    outs = [floats(rows, width)] * 2 + [floats(rows // 2, width)] * 2 + [floats(rows, width)]
    scratch = [
        pltpu.VMEM((rows, 2 * depth), jnp.bfloat16),
        pltpu.VMEM((RING, 2 * depth, width), jnp.bfloat16),
        pltpu.VMEM((RING, rows, width), jnp.float32),
        pltpu.SemaphoreType.DMA((27,)),
        pltpu.SemaphoreType.DMA((5,)),
    ]
    flops = 4 * RING * rows * depth * width
    operands = (delta, *acts, *blocks_0, *blocks_1)
    return call(forward_kernel, outs, (where,), operands, scratch, flops, 24 * MIB)


def backward(own, where, delta, cot, blocks_0, blocks_1):
    _, rows, depth = delta.shape
    width = RING * cot.shape[2]
    outs = [floats(rows // 2, depth)] * 2
    scratch = [
        pltpu.VMEM((rows, width), jnp.bfloat16),
        pltpu.VMEM((depth, width), jnp.bfloat16),
        pltpu.VMEM((rows, depth), jnp.float32),
        pltpu.SemaphoreType.DMA((3 * CHUNKS * RING,)),
        pltpu.SemaphoreType.DMA((2,)),
    ]
    flops = 2 * rows * depth * width
    operands = (delta, cot, *blocks_0, *blocks_1)
    return call(functools.partial(backward_kernel, own), outs, (where,), operands, scratch, flops, 16 * MIB)


def tie(*values):
    return lax.optimization_barrier(values)


def near(block, axis):
    return shift(block, axis, -1), shift(block, axis, 1)


def far(following, previous, axis):
    half = following.shape[0] // 2
    top = shift(previous[:half], axis, 1)
    bottom = shift(following[half:], axis, -1)
    return top, bottom


def merge(up, down, got):
    from_before, from_after = got
    half = up.shape[0] // 2
    up = up.at[:half].add(from_before)
    down = down.at[half:].add(from_after)
    return up, down


def local(acts, frozen, delta_tiles, delta_index, delta_count, cotangent):
    x, zl, core, y, zh = (lax.axis_index(a) for a in AXES)
    tokens, width = acts.shape
    per_owner, size = delta_tiles.shape[1], delta_tiles.shape[2]
    half_width = width // 2
    step = half_width // CHUNKS
    scaling = 1.0 / math.sqrt(tokens * RING * 4)
    where = jnp.stack([x, zl, core, zh, y]).astype(jnp.int32)
    own_is_b = zh == zl

    left, right = cotangent[:, :half_width], cotangent[:, half_width:]
    keep = jnp.where(core == 0, left, right)
    give = jnp.where(core == 0, right, left)

    def along_z(block):
        part_0 = lax.ppermute(block, ("zl", "zh"), [(0, 2), (1, 0), (2, 3), (3, 1)])
        part_1 = lax.ppermute(block, ("zl", "zh"), [(1, 2), (2, 1)])
        return part_0, part_1

    def parts(block, pair):
        return pair[0], jnp.where(own_is_b, block, pair[1])

    live = jnp.arange(per_owner, dtype=jnp.int32) < delta_count[0, 0]
    info = jnp.concatenate([delta_index[0], live[:, None].astype(jnp.int32)], axis=1)
    info = jnp.pad(info[:, None, :], ((0, 0), (0, EXTRA - 1), (0, size - 3)))
    mine = jnp.concatenate([delta_tiles[0] * live[:, None, None].astype(jnp.bfloat16), info.astype(jnp.bfloat16)], axis=1)

    frozen_0, frozen_1 = frozen[:, :step], frozen[:, step:]
    got_z = along_z(frozen_0)
    next_1, prev_1 = near(frozen_1, "x")
    far_1 = far(next_1, prev_1, "x")
    cot_rows = jnp.concatenate([keep, swap(give, "core")], axis=0)
    pair = jnp.concatenate([mine, swap(mine, "zh")], axis=0)
    other_pair = swap(pair, "zl")
    acts, frozen_0, got_z, pair, other_pair, cot_rows, frozen_1, next_1, far_1, prev_1 = tie(
        acts, frozen_0, got_z, pair, other_pair, cot_rows, frozen_1, next_1, far_1, prev_1
    )

    quad = jnp.concatenate([jnp.where(zl == 0, pair, other_pair), jnp.where(zl == 0, other_pair, pair)], axis=0)
    tiles = lax.all_gather(quad, ("x", "core"), axis=0, tiled=True)
    rest_1 = jnp.stack([next_1, jnp.concatenate(far_1, axis=0)])
    got_first = along_z(frozen_1)
    acts_other = swap(acts, "zh")
    cot_next, cot_prev = near(cot_rows, "y")
    cot_far = jnp.concatenate(far(cot_next, cot_prev, "y"), axis=0)
    cot_rows, cot_next, cot_far, cot_prev, frozen_0, got_z, got_first, rest_1 = tie(
        cot_rows, cot_next, cot_far, cot_prev, frozen_0, got_z, got_first, rest_1
    )

    piece_0 = jnp.concatenate(parts(frozen_0, got_z), axis=0)
    next_0, prev_0 = near(piece_0, "x")
    got_rest = along_z(rest_1)
    swapped = swap(jnp.stack([acts, acts_other]), "core")
    cot = jnp.stack([cot_rows, cot_next, cot_far, cot_prev])
    codes = slot_codes(where, tiles[:, size, :3].astype(jnp.int32))
    slots = codes.shape[0]
    acts_all = (acts, acts_other, swapped)
    scalars = (where, codes)
    delta_back, own_grads, other_grads = slot_backward(scalars, tiles, cot, acts_all)
    next_0, prev_0, got_rest, prev_1, delta_back, own_grads, other_grads, cot, acts_all = tie(
        next_0, prev_0, got_rest, prev_1, delta_back, own_grads, other_grads, cot, acts_all
    )
    far_0 = far(next_0, prev_0, "x")
    got_last = along_z(prev_1)
    swapped_grads = swap(other_grads, "core")
    delta_out = slot_forward(scalars, tiles, acts_all, half_width)
    delta_out, own_grads, swapped_grads, far_0, got_last, acts_all = tie(
        delta_out, own_grads, swapped_grads, far_0, got_last, acts_all
    )

    def slab(k):
        place = ((x + k) % RING) * (slots // 8)
        return lax.dynamic_slice_in_dim(own_grads, place, slots // 8, 0) + lax.dynamic_slice_in_dim(
            swapped_grads, place, slots // 8, 0
        )

    eighth = slots // 16
    blocks_0 = (piece_0, next_0, *far_0, prev_0)
    blocks_1 = (frozen_1, rest_1, prev_1, *got_first, *got_rest, *got_last)
    far_slab = slab(2)
    got_g = shift(far_slab[:eighth], "x", 1), shift(far_slab[eighth:], "x", -1)
    other_keep, other_give = backward(False, where, delta_back, cot, blocks_0, blocks_1)
    other_keep, other_give, delta_out = tie(other_keep, other_give, delta_out)
    other_given = swap(other_give, "core")
    mine_out, up, far_top, far_bottom, down = forward(where, delta_out, acts_all, blocks_0, blocks_1)
    mine_out, up, far_top, far_bottom, down, got_g, other_keep, other_given = tie(
        mine_out, up, far_top, far_bottom, down, got_g, other_keep, other_given
    )

    got = shift(far_top, "y", 1), shift(far_bottom, "y", -1)
    up_g, down_g = merge(slab(1), slab(3), got_g)
    got_g = shift(up_g, "x", 1), shift(down_g, "x", -1)
    back_got = swap(other_keep + other_given, "zh")
    own_keep, own_give = backward(True, where, delta_back, cot, blocks_0, blocks_1)
    got, up, down, own_keep, own_give = tie(got, up, down, own_keep, own_give)

    up, down = merge(up, down, got)
    got = shift(up, "y", 1), shift(down, "y", -1)
    back_own = own_keep + swap(own_give, "core")

    grads = slab(0) + got_g[0] + got_g[1]
    grads, back_got = tie(grads, back_got)
    grads_zl = grads.reshape(2, -1, size, size)
    grads = lax.dynamic_index_in_dim(grads_zl, zl, 0, keepdims=False) + swap(
        lax.dynamic_index_in_dim(grads_zl, 1 - zl, 0, keepdims=False), "zl"
    )
    grad_input = (back_own + back_got).astype(jnp.bfloat16)
    grads, grad_input = tie(grads, grad_input)
    grads = grads[:per_owner] + swap(grads[per_owner:], "zh")
    delta_grad = (grads * scaling * live[:, None, None].astype(jnp.float32))[None]

    mine_out = (mine_out + got[0] + got[1]).astype(jnp.bfloat16)
    kept, got = mine_out[:tokens], swap(mine_out[tokens:], "core")
    output = jnp.concatenate([jnp.where(core == 0, kept, got), jnp.where(core == 0, got, kept)], axis=1)
    return output, grad_input, delta_grad


def solution(mesh):
    fine = Mesh(mesh.devices.reshape(4, 2, 2, 4, 2), AXES)
    rows, cols = ("x", "zl", "core"), ("y", "zh")
    return jax.shard_map(
        local,
        mesh=fine,
        in_specs=(
            P(rows, cols),
            P(cols, rows),
            P(cols, rows, None, None),
            P(cols, rows, None),
            P(cols, rows),
            P(rows, cols),
        ),
        out_specs=(P(rows, cols), P(rows, cols), P(cols, rows, None, None)),
        check_vma=False,
    )
```

```python
import functools
import math

import jax
import jax.numpy as jnp
from jax import lax
from jax.experimental import pallas as pl
from jax.experimental.pallas import tpu as pltpu
from jax.sharding import Mesh, PartitionSpec as P

AXES = ("x", "zl", "core", "y", "zh")
RING = 4
CHUNKS = 2
EXTRA = 16
COST = 1000
VMEM_LIMIT = 60 * 1024 * 1024


def shift(value, axis, step):
    return lax.ppermute(value, axis, [(i, (i + step) % RING) for i in range(RING)])


def swap(value, axis):
    return lax.ppermute(value, axis, [(0, 1), (1, 0)])


def dot(a, b):
    return jnp.dot(a, b, preferred_element_type=jnp.float32)


def dot_t(a, b):
    return lax.dot_general(a, b, (((1,), (1,)), ((), ())), preferred_element_type=jnp.float32)


def slot_codes(where, info):
    x, zl, core, zh, _ = (where[i] for i in range(5))
    row, col, live = info[:, 0], info[:, 1], info[:, 2]
    slot = jnp.arange(info.shape[0], dtype=jnp.int32)
    slice_zh = zh ^ ((slot >> 2) & 1)
    here = (live > 0) & (((col >> 3) & 1) == zh) & (((col >> 2) & 1) == core)
    ring = ((col >> 4) + RING - x) & 3
    part = 1 - (slice_zh ^ zl)
    code = (part << 8) | (row << 5) | (((col >> 1) & 1) << 4) | (ring << 2) | (col & 1)
    return jnp.where(here, code, -1)


def slot_place(code):
    return code >> 8, (code >> 5) & 7, (code >> 4) & 1, (code >> 2) & 3, code & 1


def block_at(index, size):
    return pl.ds(pl.multiple_of(index * size, size), size)


def start_all(copies, sems):
    started = []
    for i, (source, target, *choice) in enumerate(copies):
        copy = pltpu.make_async_copy(source, target, sems.at[i])
        if choice:
            flag, instead = choice
            pl.when(flag)(pltpu.make_async_copy(instead, target, sems.at[i]).start)
            pl.when(jnp.logical_not(flag))(copy.start)
        else:
            copy.start()
        started.append(copy)
    return started


def each_slot(codes_ref, tiles_ref, body):
    def one(slot, carry):
        code = codes_ref[slot]

        @pl.when(code >= 0)
        def _():
            body(slot_place(code), tiles_ref[slot])

        return carry

    lax.fori_loop(0, tiles_ref.shape[0], one, 0)


def block_copies(where_ref, refs, part, rows, target_of):
    same = where_ref[1] == where_ref[3]
    first, length = rows
    copies = []
    for ring in range(RING):
        target = target_of(ring)
        if len(refs) == 9:
            piece = (0, 1, 1, 2)[ring]
            sent, got = (
                (ref.at[ring - 1] if piece == 1 else ref).at[pl.ds(first, length)]
                for ref in (refs[piece], refs[3 + 2 * piece + part])
            )
            copies.append((got, target, same, sent) if part == 1 else (got, target))
        elif ring == 2:
            copies.append((refs[2 + part].at[pl.ds(first, length)], target))
        else:
            depth = refs[0].shape[0] // 2
            copies.append((refs[(0, 1, None, 4)[ring]].at[pl.ds(part * depth + first, length)], target))
    return copies


def clear(ref):
    def one(i, carry):
        ref[i] = jnp.zeros(ref.shape[1:], ref.dtype)
        return carry

    lax.fori_loop(0, ref.shape[0], one, 0)


def acts_copies(where_ref, refs, acts):
    own = 1 - where_ref[3] ^ where_ref[1]
    acts_ref, other_ref, swapped_ref = refs
    tokens, depth = acts_ref.shape
    rows = pl.ds(0, tokens), pl.ds(tokens, tokens)
    cols = [pl.ds(pl.multiple_of(part * depth, depth), depth) for part in (own, 1 - own)]
    return [
        (acts_ref, acts.at[rows[0], cols[0]]),
        (other_ref, acts.at[rows[0], cols[1]]),
        (swapped_ref.at[0], acts.at[rows[1], cols[0]]),
        (swapped_ref.at[1], acts.at[rows[1], cols[1]]),
    ]


def slot_forward_kernel(where_ref, codes_ref, tiles_ref, *refs):
    acts_refs, (out_ref, acts, tiles, sums, sems) = refs[:3], refs[3:]
    size = tiles.shape[2]
    rows = acts.shape[1] // size // 2
    per_chunk = sums.shape[2] // size // CHUNKS
    started = start_all([*acts_copies(where_ref, acts_refs, acts), (tiles_ref.at[:, pl.ds(0, size)], tiles)], sems)
    clear(sums)
    for copy in started:
        copy.wait()

    def add(place, tile):
        part, row, chunk, ring, col = place
        r, c = block_at(part * rows + row, size), block_at(chunk * per_chunk + col, size)
        sums[ring, :, c] += dot(acts[:, r], tile)

    each_slot(codes_ref, tiles, add)
    for copy in start_all([(sums, out_ref)], sems):
        copy.wait()


def slot_backward_kernel(where_ref, codes_ref, tiles_ref, cot_ref, *refs):
    acts_refs, (back_ref, own_ref, other_ref, acts, cot, tiles, sums, grads, sems) = refs[:3], refs[3:]
    size = tiles.shape[2]
    half = own_ref.shape[0]
    rows = acts.shape[1] // size // 2
    x, core, y = where_ref[0], where_ref[2], where_ref[4]
    copies = [*acts_copies(where_ref, acts_refs, acts), (cot_ref, cot), (tiles_ref.at[:, pl.ds(0, size)], tiles)]
    started = start_all(copies, sems)
    clear(sums)
    for copy in started:
        copy.wait()

    def fill(owner_core, first):
        def one(i, carry):
            slot = ((i >> 4) << 5) + (owner_core << 4) + (i & 15)
            code = codes_ref[slot]

            @pl.when(code >= 0)
            def _():
                part, row, chunk, ring, col = slot_place(code)
                cots = cot[(ring + x + RING - y) & 3, :, block_at(2 * chunk + col, size)]
                sums[part, :, block_at(row, size)] += dot_t(cots, tiles[slot])
                grads[first + i] = lax.dot_general(
                    acts[:, block_at(part * rows + row, size)],
                    cots,
                    (((0,), (0,)), ((), ())),
                    preferred_element_type=jnp.float32,
                )

            @pl.when(code < 0)
            def _():
                grads[first + i] = jnp.zeros((size, size), jnp.float32)

            return carry

        lax.fori_loop(0, half, one, 0)

    fill(1 - core, half)
    other_out = pltpu.make_async_copy(grads.at[pl.ds(half, half)], other_ref, sems.at[0])
    other_out.start()
    fill(core, 0)
    last = [
        pltpu.make_async_copy(grads.at[pl.ds(0, half)], own_ref, sems.at[1]),
        pltpu.make_async_copy(sums, back_ref, sems.at[2]),
    ]
    for copy in last:
        copy.start()
    for copy in (other_out, *last):
        copy.wait()


def forward_kernel(where_ref, delta_ref, *refs):
    acts_refs, blocks_0, blocks_1, rest = refs[:3], refs[3:8], refs[8:17], refs[17:]
    (mine_ref, up_ref, far_top_ref, far_bottom_ref, down_ref), (acts, blocks, sums, sems, out_sems) = rest[:5], rest[5:]
    x, y = where_ref[0], where_ref[4]
    step = sums.shape[2] // CHUNKS
    depth = blocks.shape[1] // 2
    half = acts.shape[0] // 2

    rings = [[(delta_ref.at[ring], sums.at[ring])] for ring in range(RING)]
    for chunk, chunk_refs in enumerate((blocks_0, blocks_1)):
        for part in range(2):

            def target(ring, chunk=chunk, part=part):
                return blocks.at[ring, pl.ds(part * depth, depth), pl.ds(chunk * step, step)]

            for ring, copy in enumerate(block_copies(where_ref, chunk_refs, part, (0, depth), target)):
                rings[ring].append(copy)
    each = len(rings[0])
    started = start_all(acts_copies(where_ref, acts_refs, acts) + rings[0], sems)
    for ring in range(RING):
        for copy in started:
            copy.wait()
        if ring + 1 < RING:
            started = start_all(rings[ring + 1], sems.at[pl.ds((ring % 2 + 1) * 9, each)])
        sums[ring] += dot(acts[...], blocks[ring])
        place = (x + RING + ring - y) & 3
        for k, ref in ((0, mine_ref), (1, up_ref), (3, down_ref)):
            pl.when(place == k)(pltpu.make_async_copy(sums.at[ring], ref, out_sems.at[k]).start)
        for i, ref in enumerate((far_top_ref, far_bottom_ref)):
            source = sums.at[ring, pl.ds(i * half, half)]
            pl.when(place == 2)(pltpu.make_async_copy(source, ref, out_sems.at[2 + 2 * i]).start)
    for k, ref in ((0, mine_ref), (1, up_ref), (3, down_ref), (2, far_top_ref), (4, far_bottom_ref)):
        pltpu.make_async_copy(sums.at[0, pl.ds(0, ref.shape[0])], ref, out_sems.at[k]).wait()


def backward_kernel(own, where_ref, delta_ref, cot_ref, *refs):
    blocks_0, blocks_1, rest = refs[:5], refs[5:14], refs[14:]
    (keep_ref, give_ref), (cot, blocks, sums, sems, out_sems) = rest[:2], rest[2:]
    x, zl, zh, y = where_ref[0], where_ref[1], where_ref[3], where_ref[4]
    mine = 1 - zh ^ zl if own else zh ^ zl
    step = cot_ref.shape[2] // CHUNKS
    tokens = keep_ref.shape[0]
    half = blocks.shape[0] // 2
    each = CHUNKS * RING

    def columns(n):
        return pl.ds(n * step, step)

    cots = []
    for chunk in range(CHUNKS):
        for ring in range(RING):
            source = cot_ref.at[(x + ring + RING - y) & 3, :, pl.ds(chunk * step, step)]
            cots.append((source, cot.at[:, columns(chunk * RING + ring)]))

    def start_piece(i):
        rows = pl.ds(i * half, half)
        for part in range(2):

            @pl.when(mine == part)
            def _(part=part):
                copies = []
                for chunk, chunk_refs in enumerate((blocks_0, blocks_1)):

                    def target(ring, chunk=chunk):
                        return blocks.at[rows, columns(chunk * RING + ring)]

                    copies += block_copies(where_ref, chunk_refs, part, (i * half, half), target)
                start_all(copies, sems.at[pl.ds(each * (1 + i), each)])

        waits = [pltpu.make_async_copy(delta_ref.at[mine, :, rows], sums.at[:, rows], out_sems.at[i])]
        waits[0].start()
        for n in range(each):
            target = blocks.at[rows, columns(n)]
            waits.append(pltpu.make_async_copy(target, target, sems.at[each * (1 + i) + n]))
        return waits

    started = start_all(cots, sems) + start_piece(0)
    for i in range(2):
        for copy in started:
            copy.wait()
        if i == 0:
            started = start_piece(1)
        rows = slice(i * half, (i + 1) * half)
        sums[:, rows] += dot_t(cot[...], blocks[rows])
    out = start_all([(sums.at[pl.ds(tokens, tokens)], give_ref), (sums.at[pl.ds(0, tokens)], keep_ref)], out_sems)
    for copy in out:
        copy.wait()


def floats(*shape):
    return jax.ShapeDtypeStruct(shape, jnp.float32)


def call(kernel, outs, scalars, operands, scratch, flops, moved):
    in_specs = [pl.BlockSpec(memory_space=pltpu.SMEM)] * len(scalars)
    in_specs += [pl.BlockSpec(memory_space=pl.ANY)] * len(operands)
    return pl.pallas_call(
        kernel,
        out_shape=outs,
        in_specs=in_specs,
        out_specs=[pl.BlockSpec(memory_space=pl.ANY)] * len(outs),
        scratch_shapes=scratch,
        compiler_params=pltpu.CompilerParams(vmem_limit_bytes=VMEM_LIMIT),
        cost_estimate=pl.CostEstimate(flops=flops // COST, bytes_accessed=moved // COST, transcendentals=0),
    )(*scalars, *operands)


MIB = 1024 * 1024


def slot_forward(scalars, tiles, acts, width):
    rows, depth = 2 * acts[0].shape[0], acts[0].shape[1]
    count, size = tiles.shape[0], tiles.shape[2]
    scratch = [
        pltpu.VMEM((rows, 2 * depth), jnp.bfloat16),
        pltpu.VMEM((count, size, size), jnp.bfloat16),
        pltpu.VMEM((RING, rows, width), jnp.float32),
        pltpu.SemaphoreType.DMA((5,)),
    ]
    flops = count * rows * size * size
    return call(slot_forward_kernel, [floats(RING, rows, width)], scalars, (tiles, *acts), scratch, flops, 16 * MIB)[0]


def slot_backward(scalars, tiles, cot, acts):
    rows, depth = 2 * acts[0].shape[0], acts[0].shape[1]
    count, size = tiles.shape[0], tiles.shape[2]
    outs = [floats(2, rows, depth)] + [floats(count // 2, size, size)] * 2
    scratch = [
        pltpu.VMEM((rows, 2 * depth), jnp.bfloat16),
        pltpu.VMEM(cot.shape, jnp.bfloat16),
        pltpu.VMEM((count, size, size), jnp.bfloat16),
        pltpu.VMEM((2, rows, depth), jnp.float32),
        pltpu.VMEM((count, size, size), jnp.float32),
        pltpu.SemaphoreType.DMA((6,)),
    ]
    flops = 2 * count * rows * size * size
    return call(slot_backward_kernel, outs, scalars, (tiles, cot, *acts), scratch, flops, 24 * MIB)


def forward(where, delta, acts, blocks_0, blocks_1):
    rows, depth = 2 * acts[0].shape[0], acts[0].shape[1]
    width = delta.shape[2]
    outs = [floats(rows, width)] * 2 + [floats(rows // 2, width)] * 2 + [floats(rows, width)]
    scratch = [
        pltpu.VMEM((rows, 2 * depth), jnp.bfloat16),
        pltpu.VMEM((RING, 2 * depth, width), jnp.bfloat16),
        pltpu.VMEM((RING, rows, width), jnp.float32),
        pltpu.SemaphoreType.DMA((27,)),
        pltpu.SemaphoreType.DMA((5,)),
    ]
    flops = 4 * RING * rows * depth * width
    operands = (delta, *acts, *blocks_0, *blocks_1)
    return call(forward_kernel, outs, (where,), operands, scratch, flops, 24 * MIB)


def backward(own, where, delta, cot, blocks_0, blocks_1):
    _, rows, depth = delta.shape
    width = RING * cot.shape[2]
    outs = [floats(rows // 2, depth)] * 2
    scratch = [
        pltpu.VMEM((rows, width), jnp.bfloat16),
        pltpu.VMEM((depth, width), jnp.bfloat16),
        pltpu.VMEM((rows, depth), jnp.float32),
        pltpu.SemaphoreType.DMA((3 * CHUNKS * RING,)),
        pltpu.SemaphoreType.DMA((2,)),
    ]
    flops = 2 * rows * depth * width
    operands = (delta, cot, *blocks_0, *blocks_1)
    return call(functools.partial(backward_kernel, own), outs, (where,), operands, scratch, flops, 16 * MIB)


def tie(*values):
    return lax.optimization_barrier(values)


def near(block, axis):
    return shift(block, axis, -1), shift(block, axis, 1)


def far(following, previous, axis):
    half = following.shape[0] // 2
    top = shift(previous[:half], axis, 1)
    bottom = shift(following[half:], axis, -1)
    return top, bottom


def merge(up, down, got):
    from_before, from_after = got
    half = up.shape[0] // 2
    up = up.at[:half].add(from_before)
    down = down.at[half:].add(from_after)
    return up, down


def local(acts, frozen, delta_tiles, delta_index, delta_count, cotangent):
    x, zl, core, y, zh = (lax.axis_index(a) for a in AXES)
    tokens, width = acts.shape
    per_owner, size = delta_tiles.shape[1], delta_tiles.shape[2]
    half_width = width // 2
    step = half_width // CHUNKS
    scaling = 1.0 / math.sqrt(tokens * RING * 4)
    where = jnp.stack([x, zl, core, zh, y]).astype(jnp.int32)
    own_is_b = zh == zl

    left, right = cotangent[:, :half_width], cotangent[:, half_width:]
    keep = jnp.where(core == 0, left, right)
    give = jnp.where(core == 0, right, left)

    def along_z(block):
        part_0 = lax.ppermute(block, ("zl", "zh"), [(0, 2), (1, 0), (2, 3), (3, 1)])
        part_1 = lax.ppermute(block, ("zl", "zh"), [(1, 2), (2, 1)])
        return part_0, part_1

    def parts(block, pair):
        return pair[0], jnp.where(own_is_b, block, pair[1])

    live = jnp.arange(per_owner, dtype=jnp.int32) < delta_count[0, 0]
    info = jnp.concatenate([delta_index[0], live[:, None].astype(jnp.int32)], axis=1)
    info = jnp.pad(info[:, None, :], ((0, 0), (0, EXTRA - 1), (0, size - 3)))
    mine = jnp.concatenate([delta_tiles[0] * live[:, None, None].astype(jnp.bfloat16), info.astype(jnp.bfloat16)], axis=1)

    frozen_0, frozen_1 = frozen[:, :step], frozen[:, step:]
    got_z = along_z(frozen_0)
    next_1, prev_1 = near(frozen_1, "x")
    far_1 = far(next_1, prev_1, "x")
    cot_rows = jnp.concatenate([keep, swap(give, "core")], axis=0)
    pair = jnp.concatenate([mine, swap(mine, "zh")], axis=0)
    other_pair = swap(pair, "zl")
    acts, frozen_0, got_z, pair, other_pair, cot_rows, frozen_1, next_1, far_1, prev_1 = tie(
        acts, frozen_0, got_z, pair, other_pair, cot_rows, frozen_1, next_1, far_1, prev_1
    )

    quad = jnp.concatenate([jnp.where(zl == 0, pair, other_pair), jnp.where(zl == 0, other_pair, pair)], axis=0)
    tiles = lax.all_gather(quad, ("x", "core"), axis=0, tiled=True)
    rest_1 = jnp.stack([next_1, jnp.concatenate(far_1, axis=0)])
    got_first = along_z(frozen_1)
    acts_other = swap(acts, "zh")
    cot_next, cot_prev = near(cot_rows, "y")
    cot_far = jnp.concatenate(far(cot_next, cot_prev, "y"), axis=0)
    cot_rows, cot_next, cot_far, cot_prev, frozen_0, got_z, got_first, rest_1 = tie(
        cot_rows, cot_next, cot_far, cot_prev, frozen_0, got_z, got_first, rest_1
    )

    piece_0 = jnp.concatenate(parts(frozen_0, got_z), axis=0)
    next_0, prev_0 = near(piece_0, "x")
    got_rest = along_z(rest_1)
    swapped = swap(jnp.stack([acts, acts_other]), "core")
    cot = jnp.stack([cot_rows, cot_next, cot_far, cot_prev])
    codes = slot_codes(where, tiles[:, size, :3].astype(jnp.int32))
    slots = codes.shape[0]
    acts_all = (acts, acts_other, swapped)
    scalars = (where, codes)
    delta_back, own_grads, other_grads = slot_backward(scalars, tiles, cot, acts_all)
    next_0, prev_0, got_rest, prev_1, delta_back, own_grads, other_grads, cot, acts_all = tie(
        next_0, prev_0, got_rest, prev_1, delta_back, own_grads, other_grads, cot, acts_all
    )
    far_0 = far(next_0, prev_0, "x")
    got_last = along_z(prev_1)
    swapped_grads = swap(other_grads, "core")
    delta_out = slot_forward(scalars, tiles, acts_all, half_width)
    delta_out, own_grads, swapped_grads, far_0, got_last, acts_all = tie(
        delta_out, own_grads, swapped_grads, far_0, got_last, acts_all
    )

    def slab(k):
        place = ((x + k) % RING) * (slots // 8)
        return lax.dynamic_slice_in_dim(own_grads, place, slots // 8, 0) + lax.dynamic_slice_in_dim(
            swapped_grads, place, slots // 8, 0
        )

    eighth = slots // 16
    blocks_0 = (piece_0, next_0, *far_0, prev_0)
    blocks_1 = (frozen_1, rest_1, prev_1, *got_first, *got_rest, *got_last)
    far_slab = slab(2)
    got_g = shift(far_slab[:eighth], "x", 1), shift(far_slab[eighth:], "x", -1)
    other_keep, other_give = backward(False, where, delta_back, cot, blocks_0, blocks_1)
    other_keep, other_give, delta_out = tie(other_keep, other_give, delta_out)
    other_given = swap(other_give, "core")
    mine_out, up, far_top, far_bottom, down = forward(where, delta_out, acts_all, blocks_0, blocks_1)
    mine_out, up, far_top, far_bottom, down, got_g, other_keep, other_given = tie(
        mine_out, up, far_top, far_bottom, down, got_g, other_keep, other_given
    )

    got = shift(far_top, "y", 1), shift(far_bottom, "y", -1)
    up_g, down_g = merge(slab(1), slab(3), got_g)
    got_g = shift(up_g, "x", 1), shift(down_g, "x", -1)
    back_got = swap(other_keep + other_given, "zh")
    own_keep, own_give = backward(True, where, delta_back, cot, blocks_0, blocks_1)
    got, up, down, own_keep, own_give = tie(got, up, down, own_keep, own_give)

    up, down = merge(up, down, got)
    got = shift(up, "y", 1), shift(down, "y", -1)
    back_own = own_keep + swap(own_give, "core")

    grads = slab(0) + got_g[0] + got_g[1]
    grads, back_got = tie(grads, back_got)
    grads_zl = grads.reshape(2, -1, size, size)
    grads = lax.dynamic_index_in_dim(grads_zl, zl, 0, keepdims=False) + swap(
        lax.dynamic_index_in_dim(grads_zl, 1 - zl, 0, keepdims=False), "zl"
    )
    grad_input = (back_own + back_got).astype(jnp.bfloat16)
    grads, grad_input = tie(grads, grad_input)
    grads = grads[:per_owner] + swap(grads[per_owner:], "zh")
    delta_grad = (grads * scaling * live[:, None, None].astype(jnp.float32))[None]

    leaving = (mine_out[tokens:] + got[0][tokens:] + got[1][tokens:]).astype(jnp.bfloat16)
    kept, got = (mine_out[:tokens] + got[0][:tokens] + got[1][:tokens]).astype(jnp.bfloat16), swap(leaving, "core")
    output = jnp.concatenate([jnp.where(core == 0, kept, got), jnp.where(core == 0, got, kept)], axis=1)
    return output, grad_input, delta_grad


def solution(mesh):
    fine = Mesh(mesh.devices.reshape(4, 2, 2, 4, 2), AXES)
    rows, cols = ("x", "zl", "core"), ("y", "zh")
    return jax.shard_map(
        local,
        mesh=fine,
        in_specs=(
            P(rows, cols),
            P(cols, rows),
            P(cols, rows, None, None),
            P(cols, rows, None),
            P(cols, rows),
            P(rows, cols),
        ),
        out_specs=(P(rows, cols), P(rows, cols), P(cols, rows, None, None)),
        check_vma=False,
    )
```
